256 devices in a mesh: gx: 16 (over z, x_lo), gy: 2 (over core), gz: 8 (over y, x_hi).
Axes of the slice: x: 4 (x_hi: 2, x_lo: 2; x = x_hi * 2 + x_lo), y: 4, z: 8, core: 2. Of those that a mesh axis runs over, the one named last changes fastest.
Arguments:
- field: bfloat16 [32, 384, 96, 1024], P(None, 'gx', 'gy', 'gz'), may hold values from -6 to 6
- start_first: float32 [384, 64], replicated, may hold values from -0.3125 to 0.3125
- factor_second: bfloat16 [96, 64], replicated, may hold values from -0.625 to 0.625
- factor_third: bfloat16 [1024, 64], replicated, may hold values from -0.1875 to 0.1875
- factor_vars: bfloat16 [32, 16], replicated, may hold values from -1 to 1
Outputs:
- first_factor: float32 [384, 64], replicated
- core: float32 [64, 64, 64, 16], P('gx', 'gy', 'gz')
The draws below stay inside these ranges and needn't reach their ends.
All inputs are finite; a program needn't handle non-finite values.
Results may differ from the reference program's by a relative error of at most 0.0031.
Values sent between devices are 32-bit elements; how exact they have to be, the bound alone decides.
No kernel may reach another device: no remote copies, remote signals or barrier semaphores. Data moves between devices by JAX's collectives and lax.ppermute only.
A program may use at most 192 MiB of HBM per device.

```python
import jax
import jax.numpy as jnp
from jax import lax

V = 32
R = 64
RV = 16
SUB = 3
CX = 24
NX = 384
NY = 96
NZ = 1024


def block_scale(rng, shape, pieces, smallest, top_value):
    loudness = 1.0
    for axis_at, blocks in pieces:
        draws = jax.random.uniform(jax.random.fold_in(jax.random.fold_in(rng, 6), axis_at), (blocks,), jnp.float32, smallest / len(pieces), top_value / len(pieces))
        loudness = loudness * jnp.repeat(jnp.exp(draws), shape[axis_at] // blocks).reshape((-1,) + (1,) * (len(shape) - 1 - axis_at))
    return loudness


def centred(stream_key, dims, width, reach, shards=(), kind=jnp.bfloat16):
    entries = jax.random.normal(stream_key, dims, jnp.float32) * width
    if len(shards) > 0:
        entries = block_scale(stream_key, dims, shards, -0.22, 0.18) * entries
    return jnp.clip(entries, min=-reach, max=reach).astype(kind)


def setup_inputs(seed: int = 0) -> dict:
    arg_keys = jax.random.split(jax.random.key(seed), 6)
    field = centred(arg_keys[0], (V, NX, NY, NZ), 1.0, 6.0, ((1, 16), (2, 2), (3, 8)))
    start_first = centred(arg_keys[1], (NX, R), NX ** -0.5, 0.3125, (), jnp.float32)
    factor_second = centred(arg_keys[2], (NY, R), NY ** -0.5, 0.625)
    factor_third = centred(arg_keys[3], (NZ, R), NZ ** -0.5, 0.1875)
    factor_vars = centred(arg_keys[4], (V, RV), V ** -0.5, 1.0)
    return dict(field=field, start_first=start_first, factor_second=factor_second, factor_third=factor_third, factor_vars=factor_vars)


highest = lax.Precision.HIGHEST

def orthonormal_steps(gram_matrix, current):
    for repeat in range(SUB):
        product = jnp.dot(gram_matrix.astype(jnp.float32), current.astype(jnp.float32), precision=highest, preferred_element_type=jnp.float32)
        inner_gram = jnp.dot(product.T.astype(jnp.float32), product.astype(jnp.float32), precision=highest, preferred_element_type=jnp.float32)
        lower_factor = jnp.linalg.cholesky(inner_gram)
        current = jax.scipy.linalg.solve_triangular(lower_factor, product.T, lower=True).T
    return current

def reference(field, start_first, factor_second, factor_third, factor_vars):
    vars_wide = factor_vars.astype(jnp.float32)
    third_wide = factor_third.astype(jnp.float32)
    second_wide = factor_second.astype(jnp.float32)

    def one_block(block_index):
        slab = lax.dynamic_slice_in_dim(field, (block_index * CX).astype(jnp.int32), CX, 1)
        reduced = jnp.einsum('lijk,le->eijk', slab.astype(jnp.float32), vars_wide, precision=highest).astype(jnp.bfloat16)
        depth = jnp.einsum('eijk,kc->ceij', reduced.astype(jnp.float32), third_wide, precision=highest)
        return jnp.einsum('ceij,jb->bcei', depth, second_wide, precision=highest)
    blocks = lax.map(one_block, jnp.arange(NX // CX, dtype=jnp.int32))
    projected = jnp.transpose(blocks, (1, 2, 3, 0, 4)).reshape(R, R, RV, NX)
    columns_all = projected.reshape(R * R * RV, NX)
    gram_matrix = jnp.dot(columns_all.T.astype(jnp.float32), columns_all.astype(jnp.float32), precision=highest, preferred_element_type=jnp.float32)
    first_factor = orthonormal_steps(gram_matrix, start_first)
    core = jnp.einsum('bcei,ia->abce', projected, first_factor, precision=highest)
    return (first_factor, core)
```

```python
import functools

import jax
import jax.numpy as jnp
from jax import lax
from jax.experimental import pallas as pl
from jax.experimental.pallas import tpu as pltpu
from jax.sharding import PartitionSpec as P

SUB = 3
R = 64
RV = 16
V = 32
CX = 24
CY = 48
CZ = 128
GX = 16
GZ = 8
HALF = CX // 2
EH = RV // 2
NX = 384
IB = 4
IPB = 2
BLOCKS = ((0, 0), (0, 1), (0, 2), (1, 1), (1, 2), (2, 2))

f32 = jnp.float32
bf16 = jnp.bfloat16
highest = lax.Precision.HIGHEST


def iota(shape, dim):
    return lax.broadcasted_iota(jnp.int32, shape, dim)


def onehot(condition):
    return jnp.where(condition, 1.0, 0.0).astype(bf16)


def dot(a, b, contract=(1, 0), precision=None):
    return lax.dot_general(
        a, b, (((contract[0],), (contract[1],)), ((), ())), precision=precision, preferred_element_type=f32
    )


def depth_kernel(field_ref, third_ref, vars_ref, keep_ref, send_ref, mix_ref, cols_ref, left_ref):
    gy = lax.axis_index("gy")
    gz = lax.axis_index("gz")

    @pl.when(pl.program_id(0) == 0)
    def _():
        rows = iota((256, RV), 0)
        pick_e = onehot(((rows >> 4) + EH * gy) & (RV - 1) == iota((256, RV), 1))
        wide = dot(pick_e, vars_ref[...], (1, 1)).astype(bf16)
        spread = onehot(iota((V, 512), 0) == iota((V, 512), 1) >> 4)
        full = dot(wide, spread)
        same_j = (iota((256, 512), 0) & 15) == (iota((256, 512), 1) & 15)
        mix_ref[...] = jnp.where(same_j, full, 0.0).astype(bf16)
        third = third_ref[pl.ds(pl.multiple_of(gz * CZ, CZ), CZ), :]
        spread = onehot(iota((R, 512), 0) == iota((R, 512), 1) >> 3)
        full = dot(third, spread)
        which = iota((CZ, 512), 1) & 7
        for e in range(EH):
            cols_ref[e * CZ : (e + 1) * CZ, :] = jnp.where(which == e, full, 0.0).astype(bf16)

    mix = mix_ref[...]
    for pair in range(IB // 2):
        for jb in range(CY // 16):
            pieces = [
                field_ref[:, 2 * pair + s, jb * 16 : jb * 16 + 16, :].reshape(512, CZ) for s in range(2)
            ]
            reduced = dot(mix, jnp.concatenate(pieces, axis=1)).astype(bf16)
            for h in range(2):
                for s in range(2):
                    top = (h * IB + 2 * pair + s) * CY + jb * 16
                    for e in range(EH):
                        left_ref[top : top + 16, e * CZ : (e + 1) * CZ] = reduced[
                            (h * EH + e) * 16 : (h * EH + e + 1) * 16, s * CZ : (s + 1) * CZ
                        ]
    depth = dot(left_ref[...], cols_ref[...])
    keep_ref[...] = depth[: IB * CY].reshape(IB, CY, 512)
    send_ref[...] = depth[IB * CY :].reshape(IB, CY, 512)


def local_depth(field, factor_third, factor_vars):
    half = jax.ShapeDtypeStruct((CX, CY, 512), f32)
    block = pl.BlockSpec((IB, CY, 512), lambda i: (i, 0, 0))
    return pl.pallas_call(
        depth_kernel,
        grid=(CX // IB,),
        in_specs=[
            pl.BlockSpec((V, IB, CY, CZ), lambda i: (0, i, 0, 0)),
            pl.BlockSpec((1024, R), lambda i: (0, 0)),
            pl.BlockSpec((V, RV), lambda i: (0, 0)),
        ],
        out_specs=[block, block],
        out_shape=[half, half],
        scratch_shapes=[
            pltpu.VMEM((256, 512), bf16),
            pltpu.VMEM((1024, 512), bf16),
            pltpu.VMEM((2 * IB * CY, 1024), bf16),
        ],
        compiler_params=pltpu.CompilerParams(vmem_limit_bytes=48 * 2**20),
        cost_estimate=pl.CostEstimate(flops=8 * 10**9, bytes_accessed=14 * 2**20, transcendentals=0),
        name="depth",
    )(field, factor_third, factor_vars)


def split(x):
    high = x.astype(bf16)
    return high, (x - high.astype(f32)).astype(bf16)


def project_kernel(keep_ref, recv_ref, second_ref, out_ref, weights_ref):
    gy = lax.axis_index("gy")

    @pl.when(pl.program_id(0) == 0)
    def _():
        rows = iota((R, R), 0)
        rank = ((rows >> 1) & 1) * 32 + (rows >> 2) * 2 + (rows & 1)
        pick = onehot(rank == iota((R, R), 1))
        own = second_ref[pl.ds(pl.multiple_of(gy * CY, 16), CY), :]
        other = second_ref[pl.ds(pl.multiple_of((1 - gy) * CY, 16), CY), :]
        stacked = jnp.concatenate([own, other, own, other], axis=0)
        weights_ref[...] = dot(pick, stacked, (1, 1)).astype(bf16)

    weights = weights_ref[...]
    low_lanes = iota((R, 128), 1) < 64
    for ip in range(IPB):
        sides = []
        for s in range(2):
            keep_high, keep_low = split(keep_ref[s, ip])
            recv_high, recv_low = split(recv_ref[s, ip])
            sides.append(dot(weights, jnp.concatenate([keep_high, recv_high, keep_low, recv_low], axis=0)))
        for q in range(4):
            first = sides[0][:, q * 128 : (q + 1) * 128]
            second = sides[1][:, q * 128 : (q + 1) * 128]
            even = jnp.where(low_lanes, first, pltpu.roll(second, 64, 1))
            odd = jnp.where(low_lanes, pltpu.roll(first, 64, 1), second)
            for g in range(GX):
                out_ref[2 * q, g, ip * 4 : ip * 4 + 4, :] = even[4 * g : 4 * g + 4, :]
                out_ref[2 * q + 1, g, ip * 4 : ip * 4 + 4, :] = odd[4 * g : 4 * g + 4, :]


def local_projected(keep, recv, factor_second):
    block = pl.BlockSpec((2, IPB, CY, 512), lambda i: (0, i, 0, 0))
    return pl.pallas_call(
        project_kernel,
        grid=(HALF // IPB,),
        in_specs=[block, block, pl.BlockSpec((2 * CY, R), lambda i: (0, 0))],
        out_specs=pl.BlockSpec((GZ, GX, 4 * IPB, 128), lambda i: (0, 0, i, 0)),
        out_shape=jax.ShapeDtypeStruct((GZ, GX, 4 * HALF, 128), f32),
        scratch_shapes=[pltpu.VMEM((R, 4 * CY), bf16)],
        compiler_params=pltpu.CompilerParams(vmem_limit_bytes=48 * 2**20),
        cost_estimate=pl.CostEstimate(flops=10**9, bytes_accessed=8 * 2**20, transcendentals=0),
        name="projected",
    )(keep.reshape(2, HALF, CY, 512), recv.reshape(2, HALF, CY, 512), factor_second)


def gram_kernel(rows_ref, gram_ref, keep_ref, send_ref, columns_ref):
    gy = lax.axis_index("gy")
    low_lanes = iota((GX * HALF, 128), 1) < 64
    for t in range(2):
        first = rows_ref[pl.ds(2 * t, GX * HALF, stride=4), :]
        second = rows_ref[pl.ds(2 * t + 1, GX * HALF, stride=4), :]
        sides = (
            jnp.where(low_lanes, first, pltpu.roll(second, 64, 1)),
            jnp.where(low_lanes, pltpu.roll(first, 64, 1), second),
        )
        for s in range(2):
            for g in range(GX):
                top = g * CX + s * HALF
                columns_ref[top : top + HALF, t * 128 : (t + 1) * 128] = sides[s][g * HALF : (g + 1) * HALF, :]
    for n, (r, c) in enumerate(BLOCKS):
        gram_ref[n * 128 : (n + 1) * 128, :] = dot(
            columns_ref[r * 128 : (r + 1) * 128, :], columns_ref[c * 128 : (c + 1) * 128, :], (1, 1), highest
        )
    low, high = columns_ref[:, :128], columns_ref[:, 128:]
    keep_ref[...] = jnp.where(gy == 0, low, high)
    send_ref[...] = jnp.where(gy == 0, high, low)


def local_gram(rows):
    half = jax.ShapeDtypeStruct((NX, 128), f32)
    return pl.pallas_call(
        gram_kernel,
        out_shape=[jax.ShapeDtypeStruct((768, 128), f32), half, half],
        scratch_shapes=[pltpu.VMEM((NX, 256), f32)],
        name="gram",
    )(rows)


def invert_lower(matrix):
    row = iota((R, 128), 0)
    lane = iota((R, 128), 1)
    work = jnp.concatenate([matrix, jnp.where(iota((R, R), 0) == iota((R, R), 1), 1.0, 0.0)], axis=1)
    pivots = jnp.ones((R, 1), f32)
    for j in range(R):
        pivot_row = work[j : j + 1, :]
        pivot = work[j : j + 1, j : j + 1]
        factor = jnp.where(row[:, :1] > j, work[:, j : j + 1] / pivot, 0.0)
        pivots = jnp.where(row[:, :1] == j, pivot, pivots)
        work = work - factor * pivot_row
    return work[:, R:] * lax.rsqrt(pivots)


def factor_kernel(gram_ref, start_ref, keep_ref, recv_ref, factor_ref, core_ref, full_ref):
    gy = lax.axis_index("gy")
    for n, (r, c) in enumerate(BLOCKS):
        block = gram_ref[n * 128 : (n + 1) * 128, :]
        full_ref[r * 128 : (r + 1) * 128, c * 128 : (c + 1) * 128] = block
        if r != c:
            full_ref[c * 128 : (c + 1) * 128, r * 128 : (r + 1) * 128] = block.T
    basis = start_ref[...]
    for _ in range(SUB):
        product = dot(full_ref[...], basis, precision=highest)
        inner = dot(product, product, (0, 0), highest)
        basis = dot(product, invert_lower(inner), (1, 1), highest)
    factor_ref[...] = basis
    keep, recv = keep_ref[...], recv_ref[...]
    columns = jnp.concatenate([jnp.where(gy == 0, keep, recv), jnp.where(gy == 0, recv, keep)], axis=1)
    core_ref[...] = dot(basis, columns, (0, 0), highest)


def factor_and_core(gram, start, keep, recv):
    return pl.pallas_call(
        factor_kernel,
        out_shape=[jax.ShapeDtypeStruct((NX, R), f32), jax.ShapeDtypeStruct((R, 256), f32)],
        scratch_shapes=[pltpu.VMEM((NX, NX), f32)],
        name="factor",
    )(gram, start, keep, recv)


def swap(x):
    return lax.ppermute(x, "gy", [(0, 1), (1, 0)])


def exchange(x, axes):
    return lax.all_to_all(x, axes, 0, 0, tiled=True)


def per_device(field, start_first, factor_second, factor_third, factor_vars):
    keep, send = local_depth(field, factor_third, factor_vars)
    partial = local_projected(keep, swap(send), factor_second)
    projected = jnp.sum(exchange(partial, "gz"), axis=0)
    rows = exchange(projected, "gx").reshape(GX * HALF * 4, 128)
    gram, keep, send = local_gram(rows)
    recv = swap(send)
    gram = jnp.sum(exchange(gram.reshape(16, 48, 128), ("gy", "gz")), axis=0)
    gram = jnp.sum(exchange(jnp.broadcast_to(gram, (16, 48, 128)), "gx"), axis=0)
    gram = exchange(jnp.broadcast_to(gram, (16, 48, 128)), ("gy", "gz")).reshape(768, 128)
    first_factor, core = factor_and_core(gram, start_first, keep, recv)
    core = exchange(core.reshape(GX, 4, 256), "gx")
    core = core.reshape(GX, 4, 2, 2, 8, EH).transpose(1, 0, 3, 4, 2, 5)
    return first_factor, core.reshape(4, 32, 8, RV)


def solution(mesh):
    in_specs = (P(None, "gx", "gy", "gz"), P(), P(), P(), P())
    out_specs = (P(), P("gx", "gy", "gz", None))
    return jax.shard_map(per_device, mesh=mesh, in_specs=in_specs, out_specs=out_specs, check_vma=False)
```

```python
import jax
import jax.numpy as jnp
from jax import lax
from jax.experimental import pallas as pl
from jax.experimental.pallas import tpu as pltpu
from jax.sharding import PartitionSpec as P

SUB = 3
R = 64
RV = 16
V = 32
CX = 24
CY = 48
CZ = 128
GX = 16
GZ = 8
HALF = CX // 2
EH = RV // 2
NX = 384
IPB = 2
STEP = 4
CHUNKS = (4, 8)
BLOCKS = ((0, 0), (0, 1), (0, 2), (1, 1), (1, 2), (2, 2))

f32 = jnp.float32
bf16 = jnp.bfloat16
highest = lax.Precision.HIGHEST


def iota(shape, dim):
    return lax.broadcasted_iota(jnp.int32, shape, dim)


def onehot(condition):
    return jnp.where(condition, 1.0, 0.0).astype(bf16)


def dot(a, b, contract=(1, 0), precision=None):
    return lax.dot_general(
        a, b, (((contract[0],), (contract[1],)), ((), ())), precision=precision, preferred_element_type=f32
    )


def depth_kernel(field_ref, third_ref, vars_ref, keep_ref, send_ref, mix_ref, cols_ref, left_ref):
    gy = lax.axis_index("gy")
    gz = lax.axis_index("gz")

    @pl.when(pl.program_id(0) == 0)
    def _():
        rows = iota((256, RV), 0)
        pick_e = onehot((((rows >> 4) + EH * gy) & (RV - 1)) == iota((256, RV), 1))
        wide = dot(pick_e, vars_ref[...]).astype(bf16)
        spread = onehot(iota((V, 512), 0) == iota((V, 512), 1) >> 4)
        same_j = (iota((256, 512), 0) & 15) == (iota((256, 512), 1) & 15)
        mix_ref[...] = jnp.where(same_j, dot(wide, spread), 0.0).astype(bf16)
        third = third_ref[:, pl.ds(pl.multiple_of(gz * CZ, CZ), CZ)]
        lane = iota((R, 256), 1)
        spread = onehot(iota((R, 256), 0) == (lane >> 5) * 8 + (lane & 7))
        full = dot(third, spread, (0, 0))
        which = (iota((CZ, 256), 1) >> 3) & 3
        for e in range(4):
            cols_ref[e * CZ : (e + 1) * CZ, :] = jnp.where(which == e, full, 0.0).astype(bf16)

    mix = mix_ref[...]
    for ip in range(IPB):
        for jb in range(CY // 16):
            pieces = [field_ref[:, s, ip, jb * 16 : jb * 16 + 16, :].reshape(512, CZ) for s in range(2)]
            reduced = dot(mix, jnp.concatenate(pieces, axis=1)).astype(bf16)
            for e in range(RV):
                for s in range(2):
                    top = ((e // 4 * 2 + s) * IPB + ip) * CY + jb * 16
                    left_ref[top : top + 16, e % 4 * CZ : (e % 4 + 1) * CZ] = reduced[
                        e * 16 : e * 16 + 16, s * CZ : (s + 1) * CZ
                    ]
    cols = cols_ref[...]
    size = 2 * IPB * CY
    for n in range(4):
        depth = dot(left_ref[n * size : (n + 1) * size, :], cols).reshape(2, IPB, CY, 256)
        (keep_ref, send_ref)[n // 2][:, :, :, n % 2 * 256 : (n % 2 + 1) * 256] = depth


def local_depth(field, third, weights, first, count):
    half = jax.ShapeDtypeStruct((2, count, CY, 512), f32)
    block = pl.BlockSpec((2, IPB, CY, 512), lambda i: (0, i, 0, 0))
    return pl.pallas_call(
        depth_kernel,
        grid=(count // IPB,),
        in_specs=[
            pl.BlockSpec((V, 2, IPB, CY, CZ), lambda i: (0, 0, i + first // IPB, 0, 0)),
            pl.BlockSpec((R, 1024), lambda i: (0, 0)),
            pl.BlockSpec((RV, V), lambda i: (0, 0)),
        ],
        out_specs=[block, block],
        out_shape=[half, half],
        scratch_shapes=[
            pltpu.VMEM((256, 512), bf16),
            pltpu.VMEM((512, 256), bf16),
            pltpu.VMEM((8 * IPB * CY, 512), bf16),
        ],
        compiler_params=pltpu.CompilerParams(vmem_limit_bytes=40 * 2**20),
        cost_estimate=pl.CostEstimate(flops=count * 6 * 10**8, bytes_accessed=count * 1200000, transcendentals=0),
        name="depth",
    )(field, third, weights)


def split(x):
    high = x.astype(bf16)
    return high, (x - high.astype(f32)).astype(bf16)


def project_kernel(keep_ref, recv_ref, second_ref, out_ref, weights_ref):
    gy = lax.axis_index("gy")

    @pl.when(pl.program_id(0) == 0)
    def _():
        rows = iota((R, R), 0)
        rank = ((rows >> 1) & 1) * 32 + (rows & 1) * 16 + (rows >> 2)
        picked = dot(onehot(rank == iota((R, R), 1)), second_ref[...])
        swapped = jnp.concatenate([picked[:, CY:], picked[:, :CY]], axis=1)
        own = jnp.where(gy == 0, picked, swapped)
        weights_ref[...] = jnp.concatenate([own, own], axis=1).astype(bf16)

    weights = weights_ref[...]
    slot = iota((R, 128), 1) >> 5
    for ip in range(IPB):
        sides = []
        for s in range(2):
            keep_high, keep_low = split(keep_ref[s, ip])
            recv_high, recv_low = split(recv_ref[s, ip])
            sides.append(dot(weights, jnp.concatenate([keep_high, recv_high, keep_low, recv_low], axis=0)))
        for t in range(2):
            tiles = [sides[n // 2][:, n % 2 * 256 + t * 128 : n % 2 * 256 + (t + 1) * 128] for n in range(4)]
            for d in range(4):
                whole = tiles[0] if d == 0 else pltpu.roll(tiles[0], (128 - 32 * d) % 128, 1)
                for n in range(1, 4):
                    shift = 32 * (n - d) % 128
                    whole = jnp.where(slot == n, tiles[n] if shift == 0 else pltpu.roll(tiles[n], shift, 1), whole)
                for g in range(GX):
                    out_ref[4 * t + d, g, ip * 4 : ip * 4 + 4, :] = whole[4 * g : 4 * g + 4, :]


def local_projected(keep, recv, second):
    count = keep.shape[1]
    block = pl.BlockSpec((2, IPB, CY, 512), lambda i: (0, i, 0, 0))
    return pl.pallas_call(
        project_kernel,
        grid=(count // IPB,),
        in_specs=[block, block, pl.BlockSpec((R, 2 * CY), lambda i: (0, 0))],
        out_specs=pl.BlockSpec((GZ, GX, 4 * IPB, 128), lambda i: (0, 0, i, 0)),
        out_shape=jax.ShapeDtypeStruct((GZ, GX, 4 * count, 128), f32),
        scratch_shapes=[pltpu.VMEM((R, 4 * CY), bf16)],
        compiler_params=pltpu.CompilerParams(vmem_limit_bytes=40 * 2**20),
        cost_estimate=pl.CostEstimate(flops=count * 10**8, bytes_accessed=count * 700000, transcendentals=0),
        name="projected",
    )(keep, recv, second)


def gram_kernel(rows_ref, gram_ref, keep_ref, send_ref, columns_ref):
    gy = lax.axis_index("gy")
    low_lanes = iota((GX * HALF, 128), 1) < 64
    for t in range(2):
        first = rows_ref[pl.ds(2 * t, GX * HALF, stride=4), :]
        second = rows_ref[pl.ds(2 * t + 1, GX * HALF, stride=4), :]
        sides = (
            jnp.where(low_lanes, first, pltpu.roll(second, 64, 1)),
            jnp.where(low_lanes, pltpu.roll(first, 64, 1), second),
        )
        for s in range(2):
            for g in range(GX):
                top = g * CX + s * HALF
                columns_ref[top : top + HALF, t * 128 : (t + 1) * 128] = sides[s][g * HALF : (g + 1) * HALF, :]
    for n, (r, c) in enumerate(BLOCKS):
        gram_ref[n * 128 : (n + 1) * 128, :] = dot(
            columns_ref[r * 128 : (r + 1) * 128, :], columns_ref[c * 128 : (c + 1) * 128, :], (1, 1), highest
        )
    low, high = columns_ref[:, :128], columns_ref[:, 128:]
    keep_ref[...] = jnp.where(gy == 0, low, high)
    send_ref[...] = jnp.where(gy == 0, high, low)


def local_gram(rows):
    half = jax.ShapeDtypeStruct((NX, 128), f32)
    return pl.pallas_call(
        gram_kernel,
        out_shape=[jax.ShapeDtypeStruct((768, 128), f32), half, half],
        scratch_shapes=[pltpu.VMEM((NX, 256), f32)],
        name="gram",
    )(rows)


def split3(x):
    high = x.astype(bf16)
    rest = x - high.astype(f32)
    middle = rest.astype(bf16)
    return high, middle, (rest - middle.astype(f32)).astype(bf16)


def dot3(left, right, contract=(1, 0)):
    n = left[0].shape[0]
    all3 = dot(jnp.concatenate(left, axis=0), right[0], contract)
    two = dot(jnp.concatenate(left[:2], axis=0), right[1], contract)
    one = dot(left[0], right[2], contract)
    return all3[:n] + (all3[n : 2 * n] + two[:n]) + (all3[2 * n :] + two[n:] + one)


def invert_lower(matrix):
    row = iota((R, 128), 0)
    work = jnp.concatenate([matrix, jnp.where(iota((R, R), 0) == iota((R, R), 1), 1.0, 0.0)], axis=1)
    done = []
    for p in range(0, R, STEP):
        base = p // 8 * 8
        below = work[base:]
        columns = [jnp.broadcast_to(below[:, p + t : p + t + 1], below.shape) for t in range(STEP)]
        rows = [work[p + t : p + t + 1] for t in range(STEP)]
        for t in range(STEP):
            at = p + t - base
            pivot = columns[t][at : at + 1]
            inverse = 1.0 / pivot
            done.append(rows[t] * lax.rsqrt(pivot))
            scaled = rows[t] * inverse
            for s in range(t + 1, STEP):
                rows[s] = rows[s] - columns[t][p + s - base : p + s - base + 1] * scaled
                columns[s] = columns[s] - columns[t] * (columns[s][at : at + 1] * inverse)
            below = below - columns[t] * scaled
        work = below if base == 0 else jnp.concatenate([work[:base], below], axis=0)
    return jnp.concatenate(done, axis=0)[:, R:]


def factor_kernel(gram_ref, start_ref, keep_ref, recv_ref, factor_ref, core_ref, high_ref, middle_ref, low_ref):
    gy = lax.axis_index("gy")
    parts_refs = (high_ref, middle_ref, low_ref)
    for n, (r, c) in enumerate(BLOCKS):
        block = gram_ref[n * 128 : (n + 1) * 128, :]
        for ref, part in zip(parts_refs, split3(block)):
            ref[r * 128 : (r + 1) * 128, c * 128 : (c + 1) * 128] = part
        if r != c:
            for ref, part in zip(parts_refs, split3(block.T)):
                ref[c * 128 : (c + 1) * 128, r * 128 : (r + 1) * 128] = part
    gram = tuple(ref[...] for ref in parts_refs)
    basis = start_ref[...]
    for _ in range(SUB):
        product = dot3(split3(basis), gram)
        parts = split3(product)
        inner = dot3(parts, parts, (1, 1))
        basis = dot3(split3(invert_lower(inner)), parts)
    factor_ref[...] = basis
    keep, recv = keep_ref[...], recv_ref[...]
    low, high = jnp.where(gy == 0, keep, recv), jnp.where(gy == 0, recv, keep)
    low_lanes = iota((NX, 128), 1) < 64
    columns = (
        jnp.where(low_lanes, low, pltpu.roll(high, 64, 1)),
        jnp.where(low_lanes, pltpu.roll(low, 64, 1), high),
    )
    left = split(basis)
    for b in range(2):
        right = split(columns[b])
        both = dot(jnp.concatenate(left, axis=0), right[0])
        core = both[:R] + both[R:] + dot(left[0], right[1])
        for g in range(GX):
            core_ref[g, 4 * b : 4 * b + 4, :] = core[4 * g : 4 * g + 4, :]


def factor_and_core(gram, start, keep, recv):
    return pl.pallas_call(
        factor_kernel,
        out_shape=[jax.ShapeDtypeStruct((R, NX), f32), jax.ShapeDtypeStruct((GX, 8, 128), f32)],
        scratch_shapes=[pltpu.VMEM((NX, NX), bf16)] * 3,
        name="factor",
    )(gram, start, keep, recv)


def order_kernel(core_ref, out_ref, turned_ref):
    for a in range(4):
        pieces = [core_ref[pl.ds(4 * b + a, GX, stride=8), :] for b in range(2)]
        turned_ref[...] = jnp.concatenate(pieces, axis=0).T
        for c in range(8):
            out_ref[a, c] = turned_ref[pl.ds(c, RV, stride=8), :]


def ordered(core):
    out = pl.pallas_call(
        order_kernel,
        out_shape=jax.ShapeDtypeStruct((4, 8, RV, 32), f32),
        scratch_shapes=[pltpu.VMEM((128, 32), f32)],
        name="order",
    )(core.reshape(GX * 8, 128))
    return out.transpose(0, 3, 1, 2)


def swap(x):
    return lax.ppermute(x, "gy", [(0, 1), (1, 0)])


def exchange(x, axes):
    return lax.all_to_all(x, axes, 0, 0, tiled=True)


def per_device(field, start_first, factor_second, factor_third, factor_vars):
    field = field.reshape(V, 2, HALF, CY, CZ)
    sums = []
    first = 0
    for count in CHUNKS:
        keep, send = local_depth(field, factor_third.T, factor_vars.T, first, count)
        partial = local_projected(keep, swap(send), factor_second.T)
        sums.append(jnp.sum(exchange(partial, "gz"), axis=0))
        first += count
    rows = exchange(jnp.concatenate(sums, axis=1), "gx").reshape(GX * HALF * 4, 128)
    gram, keep, send = local_gram(rows)
    recv = swap(send)
    gram = jnp.sum(exchange(gram.reshape(16, 48, 128), ("gy", "gz")), axis=0)
    gram = jnp.sum(exchange(jnp.broadcast_to(gram, (16, 48, 128)), "gx"), axis=0)
    gram = exchange(jnp.broadcast_to(gram, (16, 48, 128)), ("gy", "gz")).reshape(768, 128)
    first_factor, core = factor_and_core(gram, start_first.T, keep, recv)
    return first_factor.T, ordered(exchange(core, "gx"))


def solution(mesh):
    in_specs = (P(None, "gx", "gy", "gz"), P(), P(), P(), P())
    out_specs = (P(), P("gx", "gy", "gz", None))
    return jax.shard_map(per_device, mesh=mesh, in_specs=in_specs, out_specs=out_specs, check_vma=False)
```

```python
import jax
import jax.numpy as jnp
from jax import lax
from jax.experimental import pallas as pl
from jax.experimental.pallas import tpu as pltpu
from jax.sharding import PartitionSpec as P

SUB = 3
R = 64
RV = 16
V = 32
CX = 24
CY = 48
CZ = 128
GX = 16
GZ = 8
HALF = CX // 2
EH = RV // 2
NX = 384
IPB = 4
STEP = 16
BLOCKS = ((0, 0), (0, 1), (0, 2), (1, 1), (1, 2), (2, 2))

f32 = jnp.float32
bf16 = jnp.bfloat16
highest = lax.Precision.HIGHEST


def iota(shape, dim):
    return lax.broadcasted_iota(jnp.int32, shape, dim)


def onehot(condition):
    return jnp.where(condition, 1.0, 0.0).astype(bf16)


def dot(a, b, contract=(1, 0), precision=None):
    return lax.dot_general(
        a, b, (((contract[0],), (contract[1],)), ((), ())), precision=precision, preferred_element_type=f32
    )


def depth_kernel(
    field_ref, third_ref, vars_ref, keep_ref, send_ref, cells_ref, third_here, vars_here, mix_ref, cols_ref, left_ref, sems
):
    gy = lax.axis_index("gy")
    gz = lax.axis_index("gz")

    def fetch(chunk):
        cells = pl.ds(chunk * IPB, IPB)
        return pltpu.make_async_copy(field_ref.at[:, :, cells], cells_ref.at[:, :, cells], sems.at[chunk])

    third_part = third_ref.at[:, pl.ds(pl.multiple_of(gz * CZ, CZ), CZ)]
    third_copy = pltpu.make_async_copy(third_part, third_here, sems.at[HALF // IPB])
    vars_copy = pltpu.make_async_copy(vars_ref, vars_here, sems.at[HALF // IPB + 1])
    third_copy.start()
    vars_copy.start()
    for chunk in range(HALF // IPB):
        fetch(chunk).start()

    rows = iota((128, RV), 0)
    pick_e = onehot((((rows >> 3) + EH * gy) & (RV - 1)) == iota((128, RV), 1))
    vars_copy.wait()
    wide = dot(pick_e, vars_here[...]).astype(bf16)
    spread = onehot(iota((V, 256), 0) == iota((V, 256), 1) >> 3)
    same_j = (iota((128, 256), 0) & 7) == (iota((128, 256), 1) & 7)
    mix_ref[...] = jnp.where(same_j, dot(wide, spread), 0.0).astype(bf16)
    lane = iota((R, 256), 1)
    spread = onehot(iota((R, 256), 0) == (lane >> 5) * 8 + (lane & 7))
    third_copy.wait()
    full = dot(third_here[...], spread, (0, 0))
    which = (iota((CZ, 256), 1) >> 3) & 3
    for e in range(4):
        cols_ref[e * CZ : (e + 1) * CZ, :] = jnp.where(which == e, full, 0.0).astype(bf16)

    def step(chunk, carry):
        fetch(chunk).wait()
        mix = mix_ref[...]
        for ip in range(IPB):
            for jb in range(CY // 16):
                tiles = [cells_ref[:, s, chunk * IPB + ip, jb * 16 : jb * 16 + 16, :] for s in range(2)]
                halves = []
                for h in range(2):
                    pieces = [tile[:, h * 8 : h * 8 + 8, :].reshape(256, CZ) for tile in tiles]
                    halves.append(dot(mix, jnp.concatenate(pieces, axis=1)).reshape(RV, 8, 2 * CZ))
                reduced = jnp.concatenate(halves, axis=1).astype(bf16)
                for e in range(RV):
                    for s in range(2):
                        top = ((e // 4 * 2 + s) * IPB + ip) * CY + jb * 16
                        left_ref[chunk % 2, top : top + 16, e % 4 * CZ : (e % 4 + 1) * CZ] = reduced[
                            e, :, s * CZ : (s + 1) * CZ
                        ]
        depth = dot(left_ref[chunk % 2], cols_ref[...]).reshape(4, 2, IPB, CY, 256)
        for n in range(4):
            half = (keep_ref, send_ref)[n // 2]
            half[:, pl.ds(chunk * IPB, IPB), :, n % 2 * 256 : (n % 2 + 1) * 256] = depth[n]
        return carry

    lax.fori_loop(0, HALF // IPB, step, 0)


def local_depth(field, third, weights):
    half = jax.ShapeDtypeStruct((2, HALF, CY, 512), f32)
    far = pl.BlockSpec(memory_space=pltpu.HBM)
    near = pl.BlockSpec(memory_space=pltpu.VMEM)
    return pl.pallas_call(
        depth_kernel,
        in_specs=[far, far, far],
        out_specs=[near, near],
        out_shape=[half, half],
        scratch_shapes=[
            pltpu.VMEM((V, 2, HALF, CY, CZ), bf16),
            pltpu.VMEM((R, CZ), bf16),
            pltpu.VMEM((RV, V), bf16),
            pltpu.VMEM((128, 256), bf16),
            pltpu.VMEM((512, 256), bf16),
            pltpu.VMEM((2, 8 * IPB * CY, 512), bf16),
            pltpu.SemaphoreType.DMA((HALF // IPB + 2,)),
        ],
        compiler_params=pltpu.CompilerParams(vmem_limit_bytes=28 * 2**20),
        cost_estimate=pl.CostEstimate(flops=7 * 10**9, bytes_accessed=14 * 2**20, transcendentals=0),
        name="depth",
    )(*(pltpu.with_memory_space_constraint(x, pltpu.HBM) for x in (field, third, weights)))


def split(x):
    high = x.astype(bf16)
    return high, (x - high.astype(f32)).astype(bf16)


def turn_lanes(tiles, slot):
    skewed = []
    for k in range(4):
        mixed = tiles[-k % 4]
        for q in range(1, 4):
            mixed = jnp.where(slot == q, tiles[(q - k) % 4], mixed)
        skewed.append(mixed if k == 0 else pltpu.roll(mixed, 128 - 32 * k, 1))
    turned = []
    for d in range(4):
        whole = skewed[d]
        for n in range(1, 4):
            whole = jnp.where(slot == n, skewed[(d - n) % 4], whole)
        turned.append(whole)
    return turned


def project_kernel(keep_ref, recv_ref, second_ref, out_ref):
    gy = lax.axis_index("gy")
    rows = iota((R, R), 0)
    rank = ((rows >> 1) & 1) * 32 + (rows & 1) * 16 + (rows >> 2)
    picked = dot(onehot(rank == iota((R, R), 1)), second_ref[...])
    swapped = jnp.concatenate([picked[:, CY:], picked[:, :CY]], axis=1)
    own = jnp.where(gy == 0, picked, swapped)
    weights = jnp.concatenate([own, own], axis=1).astype(bf16)
    slot = iota((R, 128), 1) >> 5

    def step(ip, carry):
        sides = []
        for s in range(2):
            keep_high, keep_low = split(keep_ref[s, ip])
            recv_high, recv_low = split(recv_ref[s, ip])
            sides.append(dot(weights, jnp.concatenate([keep_high, recv_high, keep_low, recv_low], axis=0)))
        for t in range(2):
            tiles = [sides[n // 2][:, n % 2 * 256 + t * 128 : n % 2 * 256 + (t + 1) * 128] for n in range(4)]
            for d, tile in enumerate(turn_lanes(tiles, slot)):
                out_ref[4 * t + d, ip] = tile
        return carry

    lax.fori_loop(0, HALF, step, 0, unroll=3)


def local_projected(keep, recv, second):
    return pl.pallas_call(
        project_kernel,
        out_shape=jax.ShapeDtypeStruct((GZ, HALF, R, 128), f32),
        compiler_params=pltpu.CompilerParams(vmem_limit_bytes=16 * 2**20),
        cost_estimate=pl.CostEstimate(flops=10**9, bytes_accessed=8 * 2**20, transcendentals=0),
        name="projected",
    )(keep, recv, second)


def gram_kernel(rows_ref, gram_ref, keep_ref, send_ref, columns_ref):
    gy = lax.axis_index("gy")
    low_lanes = iota((GX * HALF, 128), 1) < 64
    for t in range(2):
        first = rows_ref[pl.ds(2 * t, GX * HALF, stride=4), :]
        second = rows_ref[pl.ds(2 * t + 1, GX * HALF, stride=4), :]
        sides = (
            jnp.where(low_lanes, first, pltpu.roll(second, 64, 1)),
            jnp.where(low_lanes, pltpu.roll(first, 64, 1), second),
        )
        for s in range(2):
            for g in range(GX):
                top = g * CX + s * HALF
                columns_ref[top : top + HALF, t * 128 : (t + 1) * 128] = sides[s][g * HALF : (g + 1) * HALF, :]
    parts = split3(columns_ref[...])
    for n, (r, c) in enumerate(BLOCKS):
        left = [part[r * 128 : (r + 1) * 128, :] for part in parts]
        right = [part[c * 128 : (c + 1) * 128, :] for part in parts]
        gram_ref[n * 128 : (n + 1) * 128, :] = dot3(left, right, (1, 1))
    low, high = columns_ref[:, :128], columns_ref[:, 128:]
    keep_ref[...] = jnp.where(gy == 0, low, high)
    send_ref[...] = jnp.where(gy == 0, high, low)


def local_gram(rows):
    half = jax.ShapeDtypeStruct((NX, 128), f32)
    return pl.pallas_call(
        gram_kernel,
        out_shape=[jax.ShapeDtypeStruct((768, 128), f32), half, half],
        scratch_shapes=[pltpu.VMEM((NX, 256), f32)],
        compiler_params=pltpu.CompilerParams(vmem_limit_bytes=8 * 2**20),
        name="gram",
    )(rows)


def split3(x):
    high = x.astype(bf16)
    rest = x - high.astype(f32)
    middle = rest.astype(bf16)
    return high, middle, (rest - middle.astype(f32)).astype(bf16)


def dot3(left, right, contract=(1, 0)):
    n = left[0].shape[0]
    all3 = dot(jnp.concatenate(left, axis=0), right[0], contract)
    two = dot(jnp.concatenate(left[:2], axis=0), right[1], contract)
    one = dot(left[0], right[2], contract)
    return all3[:n] + (all3[n : 2 * n] + two[:n]) + (all3[2 * n :] + two[n:] + one)


def invert_lower(matrix):
    row = iota((R, 128), 0)
    work = jnp.concatenate([matrix, jnp.where(iota((R, R), 0) == iota((R, R), 1), 1.0, 0.0)], axis=1)
    done = []
    for p in range(0, R, STEP):
        base = p // 8 * 8
        below = work[base:]
        columns = [jnp.broadcast_to(below[:, p + t : p + t + 1], below.shape) for t in range(STEP)]
        rows = [work[p + t : p + t + 1] for t in range(STEP)]
        for t in range(STEP):
            at = p + t - base
            pivot = columns[t][at : at + 1]
            inverse = 1.0 / pivot
            done.append(rows[t] * lax.rsqrt(pivot))
            scaled = rows[t] * inverse
            for s in range(t + 1, STEP):
                rows[s] = rows[s] - columns[t][p + s - base : p + s - base + 1] * scaled
                columns[s] = columns[s] - columns[t] * (columns[s][at : at + 1] * inverse)
            below = below - columns[t] * scaled
        work = below if base == 0 else jnp.concatenate([work[:base], below], axis=0)
    return jnp.concatenate(done, axis=0)[:, R:]


def factor_kernel(gram_ref, start_ref, keep_ref, recv_ref, factor_ref, core_ref, high_ref, middle_ref, low_ref):
    gy = lax.axis_index("gy")
    parts_refs = (high_ref, middle_ref, low_ref)
    for n, (r, c) in enumerate(BLOCKS):
        block = gram_ref[n * 128 : (n + 1) * 128, :]
        for ref, part in zip(parts_refs, split3(block)):
            ref[r * 128 : (r + 1) * 128, c * 128 : (c + 1) * 128] = part
        if r != c:
            for ref, part in zip(parts_refs, split3(block.T)):
                ref[c * 128 : (c + 1) * 128, r * 128 : (r + 1) * 128] = part
    gram = tuple(ref[...] for ref in parts_refs)
    basis = start_ref[...]
    for _ in range(SUB):
        product = dot3(split3(basis), gram)
        parts = split3(product)
        inner = dot3(parts, parts, (1, 1))
        basis = dot3(split3(invert_lower(inner)), parts)
    factor_ref[...] = basis
    keep, recv = keep_ref[...], recv_ref[...]
    low, high = jnp.where(gy == 0, keep, recv), jnp.where(gy == 0, recv, keep)
    low_lanes = iota((NX, 128), 1) < 64
    columns = (
        jnp.where(low_lanes, low, pltpu.roll(high, 64, 1)),
        jnp.where(low_lanes, pltpu.roll(low, 64, 1), high),
    )
    left = split(basis)
    for b in range(2):
        right = split(columns[b])
        both = dot(jnp.concatenate(left, axis=0), right[0])
        core = both[:R] + both[R:] + dot(left[0], right[1])
        for g in range(GX):
            core_ref[g, 4 * b : 4 * b + 4, :] = core[4 * g : 4 * g + 4, :]


def factor_and_core(gram, start, keep, recv):
    return pl.pallas_call(
        factor_kernel,
        out_shape=[jax.ShapeDtypeStruct((R, NX), f32), jax.ShapeDtypeStruct((GX, 8, 128), f32)],
        scratch_shapes=[pltpu.VMEM((NX, NX), bf16)] * 3,
        compiler_params=pltpu.CompilerParams(vmem_limit_bytes=8 * 2**20),
        name="factor",
    )(gram, start, keep, recv)


def order_kernel(core_ref, out_ref, turned_ref):
    for a in range(4):
        pieces = [core_ref[pl.ds(4 * b + a, GX, stride=8), :] for b in range(2)]
        turned_ref[...] = jnp.concatenate(pieces, axis=0).T
        for c in range(8):
            out_ref[a, c] = turned_ref[pl.ds(c, RV, stride=8), :]


def ordered(core):
    out = pl.pallas_call(
        order_kernel,
        out_shape=jax.ShapeDtypeStruct((4, 8, RV, 32), f32),
        scratch_shapes=[pltpu.VMEM((128, 32), f32)],
        compiler_params=pltpu.CompilerParams(vmem_limit_bytes=8 * 2**20),
        name="order",
    )(core.reshape(GX * 8, 128))
    return out.transpose(0, 3, 1, 2)


def swap(x):
    return lax.ppermute(x, "gy", [(0, 1), (1, 0)])


def exchange(x, axes):
    return lax.all_to_all(x, axes, 0, 0, tiled=True)


def per_device(field, start_first, factor_second, factor_third, factor_vars):
    field = field.reshape(V, 2, HALF, CY, CZ)
    keep, send = local_depth(field, factor_third.T, factor_vars.T)
    partial = local_projected(keep, swap(send), factor_second.T)
    projected = jnp.sum(exchange(partial, "gz"), axis=0)
    projected = projected.reshape(HALF, GX, 4, 128).transpose(1, 0, 2, 3).reshape(GX, HALF * 4, 128)
    rows = exchange(projected, "gx").reshape(GX * HALF * 4, 128)
    gram, keep, send = local_gram(rows)
    recv = swap(send)
    gram = jnp.sum(exchange(gram.reshape(16, 48, 128), ("gy", "gz")), axis=0)
    gram = jnp.sum(exchange(jnp.broadcast_to(gram, (16, 48, 128)), "gx"), axis=0)
    gram = exchange(jnp.broadcast_to(gram, (16, 48, 128)), ("gy", "gz")).reshape(768, 128)
    first_factor, core = factor_and_core(gram, start_first.T, keep, recv)
    return first_factor.T, ordered(exchange(core, "gx"))


def solution(mesh):
    in_specs = (P(None, "gx", "gy", "gz"), P(), P(), P(), P())
    out_specs = (P(), P("gx", "gy", "gz", None))
    return jax.shard_map(per_device, mesh=mesh, in_specs=in_specs, out_specs=out_specs, check_vma=False)
```

```python
import jax
import jax.numpy as jnp
from jax import lax
from jax.experimental import pallas as pl
from jax.experimental.pallas import tpu as pltpu
from jax.sharding import PartitionSpec as P

SUB = 3
R = 64
RV = 16
V = 32
CX = 24
CY = 48
CZ = 128
GX = 16
GZ = 8
HALF = CX // 2
EH = RV // 2
NX = 384
IPB = 4
STEP = 16
BLOCKS = ((0, 0), (0, 1), (0, 2), (1, 1), (1, 2), (2, 2))

f32 = jnp.float32
bf16 = jnp.bfloat16
highest = lax.Precision.HIGHEST


def iota(shape, dim):
    return lax.broadcasted_iota(jnp.int32, shape, dim)


def onehot(condition):
    return jnp.where(condition, 1.0, 0.0).astype(bf16)


def dot(a, b, contract=(1, 0), precision=None):
    return lax.dot_general(
        a, b, (((contract[0],), (contract[1],)), ((), ())), precision=precision, preferred_element_type=f32
    )


def depth_kernel(
    field_ref, third_ref, vars_ref, keep_ref, send_ref, cells_ref, third_here, vars_here, mix_ref, cols_ref, left_ref, sems
):
    gy = lax.axis_index("gy")
    gz = lax.axis_index("gz")

    def fetch(chunk):
        cells = pl.ds(chunk * IPB, IPB)
        return pltpu.make_async_copy(field_ref.at[:, :, cells], cells_ref.at[:, :, cells], sems.at[chunk])

    third_part = third_ref.at[:, pl.ds(pl.multiple_of(gz * CZ, CZ), CZ)]
    third_copy = pltpu.make_async_copy(third_part, third_here, sems.at[HALF // IPB])
    vars_copy = pltpu.make_async_copy(vars_ref, vars_here, sems.at[HALF // IPB + 1])
    third_copy.start()
    vars_copy.start()
    for chunk in range(HALF // IPB):
        fetch(chunk).start()

    rows = iota((128, RV), 0)
    pick_e = onehot((((rows >> 3) + EH * gy) & (RV - 1)) == iota((128, RV), 1))
    vars_copy.wait()
    wide = dot(pick_e, vars_here[...]).astype(bf16)
    spread = onehot(iota((V, 256), 0) == iota((V, 256), 1) >> 3)
    same_j = (iota((128, 256), 0) & 7) == (iota((128, 256), 1) & 7)
    mix_ref[...] = jnp.where(same_j, dot(wide, spread), 0.0).astype(bf16)
    lane = iota((R, 256), 1)
    spread = onehot(iota((R, 256), 0) == (lane >> 5) * 8 + (lane & 7))
    third_copy.wait()
    full = dot(third_here[...], spread, (0, 0))
    which = (iota((CZ, 256), 1) >> 3) & 3
    for e in range(4):
        cols_ref[e * CZ : (e + 1) * CZ, :] = jnp.where(which == e, full, 0.0).astype(bf16)

    def step(chunk, carry):
        fetch(chunk).wait()
        mix = mix_ref[...]
        for ip in range(IPB):
            for jb in range(CY // 16):
                tiles = [cells_ref[:, s, chunk * IPB + ip, jb * 16 : jb * 16 + 16, :] for s in range(2)]
                halves = []
                for h in range(2):
                    pieces = [tile[:, h * 8 : h * 8 + 8, :].reshape(256, CZ) for tile in tiles]
                    halves.append(dot(mix, jnp.concatenate(pieces, axis=1)).reshape(RV, 8, 2 * CZ))
                reduced = jnp.concatenate(halves, axis=1).astype(bf16)
                for e in range(RV):
                    for s in range(2):
                        top = ((e // 4 * 2 + s) * IPB + ip) * CY + jb * 16
                        left_ref[chunk % 2, top : top + 16, e % 4 * CZ : (e % 4 + 1) * CZ] = reduced[
                            e, :, s * CZ : (s + 1) * CZ
                        ]
        depth = dot(left_ref[chunk % 2], cols_ref[...]).reshape(4, 2, IPB, CY, 256)
        for n in range(4):
            half = (keep_ref, send_ref)[n // 2]
            half[:, pl.ds(chunk * IPB, IPB), :, n % 2 * 256 : (n % 2 + 1) * 256] = depth[n]
        return carry

    lax.fori_loop(0, HALF // IPB, step, 0)


def local_depth(field, third, weights):
    half = jax.ShapeDtypeStruct((2, HALF, CY, 512), f32)
    far = pl.BlockSpec(memory_space=pltpu.HBM)
    near = pl.BlockSpec(memory_space=pltpu.VMEM)
    return pl.pallas_call(
        depth_kernel,
        in_specs=[far, far, far],
        out_specs=[near, near],
        out_shape=[half, half],
        scratch_shapes=[
            pltpu.VMEM((V, 2, HALF, CY, CZ), bf16),
            pltpu.VMEM((R, CZ), bf16),
            pltpu.VMEM((RV, V), bf16),
            pltpu.VMEM((128, 256), bf16),
            pltpu.VMEM((512, 256), bf16),
            pltpu.VMEM((2, 8 * IPB * CY, 512), bf16),
            pltpu.SemaphoreType.DMA((HALF // IPB + 2,)),
        ],
        compiler_params=pltpu.CompilerParams(vmem_limit_bytes=28 * 2**20),
        cost_estimate=pl.CostEstimate(flops=7 * 10**9, bytes_accessed=14 * 2**20, transcendentals=0),
        name="depth",
    )(*(pltpu.with_memory_space_constraint(x, pltpu.HBM) for x in (field, third, weights)))


def split(x):
    high = x.astype(bf16)
    return high, (x - high.astype(f32)).astype(bf16)


def turn_lanes(tiles, slot):
    skewed = []
    for k in range(4):
        mixed = tiles[-k % 4]
        for q in range(1, 4):
            mixed = jnp.where(slot == q, tiles[(q - k) % 4], mixed)
        skewed.append(mixed if k == 0 else pltpu.roll(mixed, 128 - 32 * k, 1))
    turned = []
    for d in range(4):
        whole = skewed[d]
        for n in range(1, 4):
            whole = jnp.where(slot == n, skewed[(d - n) % 4], whole)
        turned.append(whole)
    return turned


def project_kernel(keep_ref, recv_ref, second_ref, across_ref, keep_out_ref, send_out_ref):
    gy = lax.axis_index("gy")
    x_half = lax.axis_index("gz") & 1
    rows = iota((R, R), 0)
    rank = ((rows >> 1) & 1) * 32 + (rows & 1) * 16 + (rows >> 2)
    picked = dot(onehot(rank == iota((R, R), 1)), second_ref[...])
    swapped = jnp.concatenate([picked[:, CY:], picked[:, :CY]], axis=1)
    own = jnp.where(gy == 0, picked, swapped)
    weights = jnp.concatenate([own, own], axis=1).astype(bf16)
    slot = iota((R, 128), 1) >> 5

    def project(ip, store):
        sides = []
        for s in range(2):
            keep_high, keep_low = split(keep_ref[s, ip])
            recv_high, recv_low = split(recv_ref[s, ip])
            sides.append(dot(weights, jnp.concatenate([keep_high, recv_high, keep_low, recv_low], axis=0)))
        for t in range(2):
            tiles = [sides[n // 2][:, n % 2 * 256 + t * 128 : n % 2 * 256 + (t + 1) * 128] for n in range(4)]
            turned = turn_lanes(tiles, slot)
            for d in range(0, 4, 2):
                own = jnp.where(x_half == 0, turned[d], turned[d + 1])
                other = jnp.where(x_half == 0, turned[d + 1], turned[d])
                store(2 * t + d // 2, own, other)

    def step(ip, carry):
        def first(y, own, other):
            across_ref[y, 0, ip] = own
            across_ref[y, 1, ip] = other

        def second(y, own, other):
            keep_out_ref[y, ip] = own
            send_out_ref[y, ip] = other

        project(ip, first)
        project(ip + HALF // 2, second)
        return carry

    lax.fori_loop(0, HALF // 2, step, 0)


def local_projected(keep, recv, second):
    part = (HALF // 2, R, 128)
    return pl.pallas_call(
        project_kernel,
        out_shape=[
            jax.ShapeDtypeStruct((4, 2, *part), f32),
            jax.ShapeDtypeStruct((4, *part), f32),
            jax.ShapeDtypeStruct((4, *part), f32),
        ],
        compiler_params=pltpu.CompilerParams(vmem_limit_bytes=16 * 2**20),
        cost_estimate=pl.CostEstimate(flops=10**9, bytes_accessed=8 * 2**20, transcendentals=0),
        name="projected",
    )(keep, recv, second)


def gram_kernel(rows_ref, keep_ref, send_ref, columns_ref):
    gy = lax.axis_index("gy")
    low_lanes = iota((GX * HALF, 128), 1) < 64
    for t in range(2):
        first = rows_ref[pl.ds(2 * t, GX * HALF, stride=4), :]
        second = rows_ref[pl.ds(2 * t + 1, GX * HALF, stride=4), :]
        sides = (
            jnp.where(low_lanes, first, pltpu.roll(second, 64, 1)),
            jnp.where(low_lanes, pltpu.roll(first, 64, 1), second),
        )
        for s in range(2):
            for g in range(GX):
                top = g * CX + s * HALF
                columns_ref[top : top + HALF, t * 128 : (t + 1) * 128] = sides[s][g * HALF : (g + 1) * HALF, :]
    parts = split3(columns_ref[...])
    blocks = []
    for r, c in BLOCKS:
        left = [part[r * 128 : (r + 1) * 128, :] for part in parts]
        right = [part[c * 128 : (c + 1) * 128, :] for part in parts]
        blocks.append(dot3(left, right, (1, 1)))
    for n in range(3):
        keep_ref[0, n * 128 : (n + 1) * 128, :] = jnp.where(gy == 0, blocks[n], blocks[n + 3])
        send_ref[0, n * 128 : (n + 1) * 128, :] = jnp.where(gy == 0, blocks[n + 3], blocks[n])
    low, high = columns_ref[:, :128], columns_ref[:, 128:]
    keep_ref[1] = jnp.where(gy == 0, low, high)
    send_ref[1] = jnp.where(gy == 0, high, low)


def local_gram(rows):
    half = jax.ShapeDtypeStruct((2, NX, 128), f32)
    return pl.pallas_call(
        gram_kernel,
        out_shape=[half, half],
        scratch_shapes=[pltpu.VMEM((NX, 256), f32)],
        compiler_params=pltpu.CompilerParams(vmem_limit_bytes=8 * 2**20),
        name="gram",
    )(rows)


def split3(x):
    high = x.astype(bf16)
    rest = x - high.astype(f32)
    middle = rest.astype(bf16)
    return high, middle, (rest - middle.astype(f32)).astype(bf16)


def dot3(left, right, contract=(1, 0)):
    n = left[0].shape[0]
    all3 = dot(jnp.concatenate(left, axis=0), right[0], contract)
    two = dot(jnp.concatenate(left[:2], axis=0), right[1], contract)
    one = dot(left[0], right[2], contract)
    return all3[:n] + (all3[n : 2 * n] + two[:n]) + (all3[2 * n :] + two[n:] + one)


def invert_lower(matrix):
    row = iota((R, 128), 0)
    work = jnp.concatenate([matrix, jnp.where(iota((R, R), 0) == iota((R, R), 1), 1.0, 0.0)], axis=1)
    done = []
    for p in range(0, R, STEP):
        base = p // 8 * 8
        below = work[base:]
        columns = [jnp.broadcast_to(below[:, p + t : p + t + 1], below.shape) for t in range(STEP)]
        rows = [work[p + t : p + t + 1] for t in range(STEP)]
        for t in range(STEP):
            at = p + t - base
            pivot = columns[t][at : at + 1]
            inverse = 1.0 / pivot
            done.append(rows[t] * lax.rsqrt(pivot))
            scaled = rows[t] * inverse
            for s in range(t + 1, STEP):
                rows[s] = rows[s] - columns[t][p + s - base : p + s - base + 1] * scaled
                columns[s] = columns[s] - columns[t] * (columns[s][at : at + 1] * inverse)
            below = below - columns[t] * scaled
        work = below if base == 0 else jnp.concatenate([work[:base], below], axis=0)
    return jnp.concatenate(done, axis=0)[:, R:]


def factor_kernel(own_ref, other_ref, start_ref, keep_ref, recv_ref, factor_ref, core_ref, high_ref, middle_ref, low_ref):
    gy = lax.axis_index("gy")
    parts_refs = (high_ref, middle_ref, low_ref)
    for n, (r, c) in enumerate(BLOCKS):
        rows = slice(n % 3 * 128, (n % 3 + 1) * 128)
        own, other = own_ref[rows, :], other_ref[rows, :]
        block = jnp.where(gy == n // 3, own, other)
        for ref, part in zip(parts_refs, split3(block)):
            ref[r * 128 : (r + 1) * 128, c * 128 : (c + 1) * 128] = part
        if r != c:
            for ref, part in zip(parts_refs, split3(block.T)):
                ref[c * 128 : (c + 1) * 128, r * 128 : (r + 1) * 128] = part
    gram = tuple(ref[...] for ref in parts_refs)
    basis = start_ref[...]
    for _ in range(SUB):
        product = dot3(split3(basis), gram)
        parts = split3(product)
        inner = dot3(parts, parts, (1, 1))
        basis = dot3(split3(invert_lower(inner)), parts)
    factor_ref[...] = basis
    keep, recv = keep_ref[1], recv_ref[1]
    low, high = jnp.where(gy == 0, keep, recv), jnp.where(gy == 0, recv, keep)
    low_lanes = iota((NX, 128), 1) < 64
    columns = (
        jnp.where(low_lanes, low, pltpu.roll(high, 64, 1)),
        jnp.where(low_lanes, pltpu.roll(low, 64, 1), high),
    )
    left = split(basis)
    for b in range(2):
        right = split(columns[b])
        both = dot(jnp.concatenate(left, axis=0), right[0])
        core = both[:R] + both[R:] + dot(left[0], right[1])
        for g in range(GX):
            core_ref[g, 4 * b : 4 * b + 4, :] = core[4 * g : 4 * g + 4, :]


def factor_and_core(own, other, start, keep, recv):
    return pl.pallas_call(
        factor_kernel,
        out_shape=[jax.ShapeDtypeStruct((R, NX), f32), jax.ShapeDtypeStruct((GX, 8, 128), f32)],
        scratch_shapes=[pltpu.VMEM((NX, NX), bf16)] * 3,
        compiler_params=pltpu.CompilerParams(vmem_limit_bytes=8 * 2**20),
        name="factor",
    )(own, other, start, keep, recv)


def order_kernel(core_ref, out_ref, turned_ref):
    for a in range(4):
        pieces = [core_ref[pl.ds(4 * b + a, GX, stride=8), :] for b in range(2)]
        turned_ref[...] = jnp.concatenate(pieces, axis=0).T
        for c in range(8):
            out_ref[a, c] = turned_ref[pl.ds(c, RV, stride=8), :]


def ordered(core):
    out = pl.pallas_call(
        order_kernel,
        out_shape=jax.ShapeDtypeStruct((4, 8, RV, 32), f32),
        scratch_shapes=[pltpu.VMEM((128, 32), f32)],
        compiler_params=pltpu.CompilerParams(vmem_limit_bytes=8 * 2**20),
        name="order",
    )(core.reshape(GX * 8, 128))
    return out.transpose(0, 3, 1, 2)


def swap(x):
    return lax.ppermute(x, "gy", [(0, 1), (1, 0)])


def swap_x(x):
    return lax.ppermute(x, "gz", [(n, n ^ 1) for n in range(GZ)])


def exchange_y(x):
    groups = [[2 * y + x for y in range(4)] for x in range(2)]
    return lax.all_to_all(x, "gz", 0, 0, tiled=True, axis_index_groups=groups)


def exchange(x, axes):
    return lax.all_to_all(x, axes, 0, 0, tiled=True)


def per_device(field, start_first, factor_second, factor_third, factor_vars):
    field = field.reshape(V, 2, HALF, CY, CZ)
    keep, send = local_depth(field, factor_third.T, factor_vars.T)
    across, keep, send = local_projected(keep, swap(send), factor_second.T)
    recv = swap_x(send)
    across = jnp.sum(exchange_y(across), axis=0)
    second = keep + recv
    recv = swap_x(across[1])
    second = jnp.sum(exchange_y(second), axis=0)
    projected = jnp.concatenate([across[0] + recv, second], axis=0)
    projected = projected.reshape(HALF, GX, 4, 128).transpose(1, 0, 2, 3).reshape(GX, HALF * 4, 128)
    rows = exchange(projected, "gx").reshape(GX * HALF * 4, 128)
    keep, send = local_gram(rows)
    recv = swap(send)
    gram = (keep[0] + recv[0]).reshape(16, 24, 128)
    gram = jnp.sum(exchange(gram, "gx"), axis=0)
    gram = jnp.sum(exchange(jnp.broadcast_to(gram, (8, 24, 128)), "gz"), axis=0)
    own = exchange(jnp.broadcast_to(gram, (16, 24, 128)), "gx").reshape(NX, 128)
    first_factor, core = factor_and_core(own, swap(own), start_first.T, keep, recv)
    return first_factor.T, ordered(exchange(core, "gx"))


def solution(mesh):
    in_specs = (P(None, "gx", "gy", "gz"), P(), P(), P(), P())
    out_specs = (P(), P("gx", "gy", "gz", None))
    return jax.shard_map(per_device, mesh=mesh, in_specs=in_specs, out_specs=out_specs, check_vma=False)
```

```python
import jax
import jax.numpy as jnp
from jax import lax
from jax.experimental import pallas as pl
from jax.experimental.pallas import tpu as pltpu
from jax.sharding import PartitionSpec as P

SUB = 3
R = 64
RV = 16
V = 32
CX = 24
CY = 48
CZ = 128
GX = 16
GZ = 8
HALF = CX // 2
EH = RV // 2
NX = 384
IPB = 4
STEP = 16
BLOCKS = ((0, 0), (0, 1), (0, 2), (1, 1), (1, 2), (2, 2))

f32 = jnp.float32
bf16 = jnp.bfloat16
highest = lax.Precision.HIGHEST


def iota(shape, dim):
    return lax.broadcasted_iota(jnp.int32, shape, dim)


def onehot(condition):
    return jnp.where(condition, 1.0, 0.0).astype(bf16)


def dot(a, b, contract=(1, 0), precision=None):
    return lax.dot_general(
        a, b, (((contract[0],), (contract[1],)), ((), ())), precision=precision, preferred_element_type=f32
    )


def depth_kernel(
    field_ref, third_ref, vars_ref, keep_ref, send_ref, cells_ref, third_here, vars_here, mix_ref, cols_ref, left_ref, sems
):
    gy = lax.axis_index("gy")
    gz = lax.axis_index("gz")

    def fetch(chunk):
        cells = pl.ds(chunk * IPB, IPB)
        return pltpu.make_async_copy(field_ref.at[:, :, cells], cells_ref.at[:, :, cells], sems.at[chunk])

    third_part = third_ref.at[:, pl.ds(pl.multiple_of(gz * CZ, CZ), CZ)]
    third_copy = pltpu.make_async_copy(third_part, third_here, sems.at[HALF // IPB])
    vars_copy = pltpu.make_async_copy(vars_ref, vars_here, sems.at[HALF // IPB + 1])
    third_copy.start()
    vars_copy.start()
    for chunk in range(HALF // IPB):
        fetch(chunk).start()

    rows = iota((128, RV), 0)
    pick_e = onehot((((rows >> 3) + EH * gy) & (RV - 1)) == iota((128, RV), 1))
    vars_copy.wait()
    wide = dot(pick_e, vars_here[...]).astype(bf16)
    spread = onehot(iota((V, 256), 0) == iota((V, 256), 1) >> 3)
    same_j = (iota((128, 256), 0) & 7) == (iota((128, 256), 1) & 7)
    mix_ref[...] = jnp.where(same_j, dot(wide, spread), 0.0).astype(bf16)
    lane = iota((R, 256), 1)
    spread = onehot(iota((R, 256), 0) == (lane >> 5) * 8 + (lane & 7))
    third_copy.wait()
    full = dot(third_here[...], spread, (0, 0))
    which = (iota((CZ, 256), 1) >> 3) & 3
    for e in range(4):
        cols_ref[e * CZ : (e + 1) * CZ, :] = jnp.where(which == e, full, 0.0).astype(bf16)

    def step(chunk, carry):
        fetch(chunk).wait()
        mix = mix_ref[...]
        for ip in range(IPB):
            for jb in range(CY // 16):
                tiles = [cells_ref[:, s, chunk * IPB + ip, jb * 16 : jb * 16 + 16, :] for s in range(2)]
                halves = []
                for h in range(2):
                    pieces = [tile[:, h * 8 : h * 8 + 8, :].reshape(256, CZ) for tile in tiles]
                    halves.append(dot(mix, jnp.concatenate(pieces, axis=1)).reshape(RV, 8, 2 * CZ))
                reduced = jnp.concatenate(halves, axis=1).astype(bf16)
                for e in range(RV):
                    for s in range(2):
                        top = ((e // 4 * 2 + s) * IPB + ip) * CY + jb * 16
                        left_ref[chunk % 2, top : top + 16, e % 4 * CZ : (e % 4 + 1) * CZ] = reduced[
                            e, :, s * CZ : (s + 1) * CZ
                        ]
        depth = dot(left_ref[chunk % 2], cols_ref[...]).reshape(4, 2, IPB, CY, 256)
        for n in range(4):
            half = (keep_ref, send_ref)[n // 2]
            half[:, pl.ds(chunk * IPB, IPB), :, n % 2 * 256 : (n % 2 + 1) * 256] = depth[n]
        return carry

    lax.fori_loop(0, HALF // IPB, step, 0)


def local_depth(field, third, weights):
    half = jax.ShapeDtypeStruct((2, HALF, CY, 512), f32)
    far = pl.BlockSpec(memory_space=pltpu.HBM)
    near = pl.BlockSpec(memory_space=pltpu.VMEM)
    return pl.pallas_call(
        depth_kernel,
        in_specs=[far, far, far],
        out_specs=[near, near],
        out_shape=[half, half],
        scratch_shapes=[
            pltpu.VMEM((V, 2, HALF, CY, CZ), bf16),
            pltpu.VMEM((R, CZ), bf16),
            pltpu.VMEM((RV, V), bf16),
            pltpu.VMEM((128, 256), bf16),
            pltpu.VMEM((512, 256), bf16),
            pltpu.VMEM((2, 8 * IPB * CY, 512), bf16),
            pltpu.SemaphoreType.DMA((HALF // IPB + 2,)),
        ],
        compiler_params=pltpu.CompilerParams(vmem_limit_bytes=28 * 2**20),
        cost_estimate=pl.CostEstimate(flops=7 * 10**9, bytes_accessed=14 * 2**20, transcendentals=0),
        name="depth",
    )(*(pltpu.with_memory_space_constraint(x, pltpu.HBM) for x in (field, third, weights)))


def split(x):
    high = x.astype(bf16)
    return high, (x - high.astype(f32)).astype(bf16)


def turn_lanes(tiles, slot):
    skewed = []
    for k in range(4):
        mixed = tiles[-k % 4]
        for q in range(1, 4):
            mixed = jnp.where(slot == q, tiles[(q - k) % 4], mixed)
        skewed.append(mixed if k == 0 else pltpu.roll(mixed, 128 - 32 * k, 1))
    turned = []
    for d in range(4):
        whole = skewed[d]
        for n in range(1, 4):
            whole = jnp.where(slot == n, skewed[(d - n) % 4], whole)
        turned.append(whole)
    return turned


def project_kernel(keep_ref, recv_ref, second_ref, across_ref, keep_out_ref, send_out_ref, across_here, sems):
    gy = lax.axis_index("gy")
    x_half = lax.axis_index("gz") & 1
    rows = iota((R, R), 0)
    rank = ((rows >> 1) & 1) * 32 + (rows & 1) * 16 + (rows >> 2)
    picked = dot(onehot(rank == iota((R, R), 1)), second_ref[...])
    swapped = jnp.concatenate([picked[:, CY:], picked[:, :CY]], axis=1)
    own = jnp.where(gy == 0, picked, swapped)
    weights = jnp.concatenate([own, own], axis=1).astype(bf16)
    slot = iota((R, 128), 1) >> 5

    def project(ip, store):
        sides = []
        for s in range(2):
            keep_high, keep_low = split(keep_ref[s, ip])
            recv_high, recv_low = split(recv_ref[s, ip])
            sides.append(dot(weights, jnp.concatenate([keep_high, recv_high, keep_low, recv_low], axis=0)))
        for t in range(2):
            tiles = [sides[n // 2][:, n % 2 * 256 + t * 128 : n % 2 * 256 + (t + 1) * 128] for n in range(4)]
            turned = turn_lanes(tiles, slot)
            for d in range(0, 4, 2):
                own = jnp.where(x_half == 0, turned[d], turned[d + 1])
                other = jnp.where(x_half == 0, turned[d + 1], turned[d])
                store(2 * t + d // 2, own, other)

    def leave(ip):
        return pltpu.make_async_copy(across_here.at[:, :, ip], across_ref.at[:, :, ip], sems.at[ip])

    def first_half(ip, carry):
        def store(y, own, other):
            across_here[y, 0, ip] = own
            across_here[y, 1, ip] = other

        project(ip, store)
        leave(ip).start()
        return carry

    def second_half(ip, carry):
        def store(y, own, other):
            keep_out_ref[y, ip] = own
            send_out_ref[y, ip] = other

        project(ip + HALF // 2, store)
        return carry

    lax.fori_loop(0, HALF // 2, first_half, 0, unroll=3)
    lax.fori_loop(0, HALF // 2, second_half, 0, unroll=3)
    for ip in range(HALF // 2):
        leave(ip).wait()


def local_projected(keep, recv, second):
    part = (HALF // 2, R, 128)
    near = pl.BlockSpec(memory_space=pltpu.VMEM)
    return pl.pallas_call(
        project_kernel,
        out_shape=[
            jax.ShapeDtypeStruct((4, 2, *part), f32),
            jax.ShapeDtypeStruct((4, *part), f32),
            jax.ShapeDtypeStruct((4, *part), f32),
        ],
        out_specs=[pl.BlockSpec(memory_space=pl.ANY), near, near],
        scratch_shapes=[pltpu.VMEM((4, 2, *part), f32), pltpu.SemaphoreType.DMA((HALF // 2,))],
        compiler_params=pltpu.CompilerParams(vmem_limit_bytes=16 * 2**20),
        cost_estimate=pl.CostEstimate(flops=10**9, bytes_accessed=8 * 2**20, transcendentals=0),
        name="projected",
    )(keep, recv, second)


def gram_kernel(rows_ref, keep_ref, send_ref, columns_ref):
    gy = lax.axis_index("gy")
    low_lanes = iota((GX * HALF, 128), 1) < 64
    for t in range(2):
        first = rows_ref[pl.ds(2 * t, GX * HALF, stride=4), :]
        second = rows_ref[pl.ds(2 * t + 1, GX * HALF, stride=4), :]
        sides = (
            jnp.where(low_lanes, first, pltpu.roll(second, 64, 1)),
            jnp.where(low_lanes, pltpu.roll(first, 64, 1), second),
        )
        for s in range(2):
            for g in range(GX):
                top = g * CX + s * HALF
                columns_ref[top : top + HALF, t * 128 : (t + 1) * 128] = sides[s][g * HALF : (g + 1) * HALF, :]
    parts = split3(columns_ref[...])
    blocks = []
    for r, c in BLOCKS:
        left = [part[r * 128 : (r + 1) * 128, :] for part in parts]
        right = [part[c * 128 : (c + 1) * 128, :] for part in parts]
        blocks.append(dot3(left, right, (1, 1)))
    for n in range(3):
        keep_ref[0, n * 128 : (n + 1) * 128, :] = jnp.where(gy == 0, blocks[n], blocks[n + 3])
        send_ref[0, n * 128 : (n + 1) * 128, :] = jnp.where(gy == 0, blocks[n + 3], blocks[n])
    low, high = columns_ref[:, :128], columns_ref[:, 128:]
    keep_ref[1] = jnp.where(gy == 0, low, high)
    send_ref[1] = jnp.where(gy == 0, high, low)


def local_gram(rows):
    half = jax.ShapeDtypeStruct((2, NX, 128), f32)
    return pl.pallas_call(
        gram_kernel,
        out_shape=[half, half],
        scratch_shapes=[pltpu.VMEM((NX, 256), f32)],
        compiler_params=pltpu.CompilerParams(vmem_limit_bytes=8 * 2**20),
        name="gram",
    )(rows)


def split3(x):
    high = x.astype(bf16)
    rest = x - high.astype(f32)
    middle = rest.astype(bf16)
    return high, middle, (rest - middle.astype(f32)).astype(bf16)


def dot3(left, right, contract=(1, 0)):
    n = left[0].shape[0]
    all3 = dot(jnp.concatenate(left, axis=0), right[0], contract)
    two = dot(jnp.concatenate(left[:2], axis=0), right[1], contract)
    one = dot(left[0], right[2], contract)
    return all3[:n] + (all3[n : 2 * n] + two[:n]) + (all3[2 * n :] + two[n:] + one)


def invert_lower(matrix):
    row = iota((R, 128), 0)
    work = jnp.concatenate([matrix, jnp.where(iota((R, R), 0) == iota((R, R), 1), 1.0, 0.0)], axis=1)
    done = []
    for p in range(0, R, STEP):
        base = p // 8 * 8
        below = work[base:]
        columns = [jnp.broadcast_to(below[:, p + t : p + t + 1], below.shape) for t in range(STEP)]
        rows = [work[p + t : p + t + 1] for t in range(STEP)]
        for t in range(STEP):
            at = p + t - base
            pivot = columns[t][at : at + 1]
            inverse = 1.0 / pivot
            done.append(rows[t] * lax.rsqrt(pivot))
            scaled = rows[t] * inverse
            for s in range(t + 1, STEP):
                rows[s] = rows[s] - columns[t][p + s - base : p + s - base + 1] * scaled
                columns[s] = columns[s] - columns[t] * (columns[s][at : at + 1] * inverse)
            below = below - columns[t] * scaled
        work = below if base == 0 else jnp.concatenate([work[:base], below], axis=0)
    return jnp.concatenate(done, axis=0)[:, R:]


def factor_kernel(own_ref, other_ref, start_ref, keep_ref, recv_ref, factor_ref, core_ref, high_ref, middle_ref, low_ref):
    gy = lax.axis_index("gy")
    parts_refs = (high_ref, middle_ref, low_ref)
    for n, (r, c) in enumerate(BLOCKS):
        rows = slice(n % 3 * 128, (n % 3 + 1) * 128)
        own, other = own_ref[rows, :], other_ref[rows, :]
        block = jnp.where(gy == n // 3, own, other)
        for ref, part in zip(parts_refs, split3(block)):
            ref[r * 128 : (r + 1) * 128, c * 128 : (c + 1) * 128] = part
        if r != c:
            for ref, part in zip(parts_refs, split3(block.T)):
                ref[c * 128 : (c + 1) * 128, r * 128 : (r + 1) * 128] = part
    gram = tuple(ref[...] for ref in parts_refs)
    basis = start_ref[...]
    for _ in range(SUB):
        product = dot3(split3(basis), gram)
        parts = split3(product)
        inner = dot3(parts, parts, (1, 1))
        basis = dot3(split3(invert_lower(inner)), parts)
    factor_ref[...] = basis
    keep, recv = keep_ref[1], recv_ref[1]
    low, high = jnp.where(gy == 0, keep, recv), jnp.where(gy == 0, recv, keep)
    low_lanes = iota((NX, 128), 1) < 64
    columns = (
        jnp.where(low_lanes, low, pltpu.roll(high, 64, 1)),
        jnp.where(low_lanes, pltpu.roll(low, 64, 1), high),
    )
    left = split(basis)
    for b in range(2):
        right = split(columns[b])
        both = dot(jnp.concatenate(left, axis=0), right[0])
        core = both[:R] + both[R:] + dot(left[0], right[1])
        for g in range(GX):
            core_ref[g, 4 * b : 4 * b + 4, :] = core[4 * g : 4 * g + 4, :]


def factor_and_core(own, other, start, keep, recv):
    return pl.pallas_call(
        factor_kernel,
        out_shape=[jax.ShapeDtypeStruct((R, NX), f32), jax.ShapeDtypeStruct((GX, 8, 128), f32)],
        scratch_shapes=[pltpu.VMEM((NX, NX), bf16)] * 3,
        compiler_params=pltpu.CompilerParams(vmem_limit_bytes=8 * 2**20),
        name="factor",
    )(own, other, start, keep, recv)


def order_kernel(core_ref, out_ref, turned_ref):
    for a in range(4):
        pieces = [core_ref[pl.ds(4 * b + a, GX, stride=8), :] for b in range(2)]
        turned_ref[...] = jnp.concatenate(pieces, axis=0).T
        for c in range(8):
            out_ref[a, c] = turned_ref[pl.ds(c, RV, stride=8), :]


def ordered(core):
    out = pl.pallas_call(
        order_kernel,
        out_shape=jax.ShapeDtypeStruct((4, 8, RV, 32), f32),
        scratch_shapes=[pltpu.VMEM((128, 32), f32)],
        compiler_params=pltpu.CompilerParams(vmem_limit_bytes=8 * 2**20),
        name="order",
    )(core.reshape(GX * 8, 128))
    return out.transpose(0, 3, 1, 2)


def swap(x):
    return lax.ppermute(x, "gy", [(0, 1), (1, 0)])


def swap_x(x):
    return lax.ppermute(x, "gz", [(n, n ^ 1) for n in range(GZ)])


def exchange_y(x):
    groups = [[2 * y + x for y in range(4)] for x in range(2)]
    return lax.all_to_all(x, "gz", 0, 0, tiled=True, axis_index_groups=groups)


def exchange(x, axes):
    return lax.all_to_all(x, axes, 0, 0, tiled=True)


def per_device(field, start_first, factor_second, factor_third, factor_vars):
    field = field.reshape(V, 2, HALF, CY, CZ)
    keep, send = local_depth(field, factor_third.T, factor_vars.T)
    across, keep, send = local_projected(keep, swap(send), factor_second.T)
    recv = swap_x(send)
    across = jnp.sum(exchange_y(across), axis=0)
    second = keep + recv
    recv = swap_x(across[1])
    second = jnp.sum(exchange_y(second), axis=0)
    projected = jnp.concatenate([across[0] + recv, second], axis=0)
    projected = projected.reshape(HALF, GX, 4, 128).transpose(1, 0, 2, 3).reshape(GX, HALF * 4, 128)
    rows = exchange(projected, "gx").reshape(GX * HALF * 4, 128)
    keep, send = local_gram(rows)
    recv = swap(send)
    gram = (keep[0] + recv[0]).reshape(16, 24, 128)
    gram = jnp.sum(exchange(gram, "gx"), axis=0)
    gram = jnp.sum(exchange(jnp.broadcast_to(gram, (8, 24, 128)), "gz"), axis=0)
    own = exchange(jnp.broadcast_to(gram, (16, 24, 128)), "gx").reshape(NX, 128)
    first_factor, core = factor_and_core(own, swap(own), start_first.T, keep, recv)
    return first_factor.T, ordered(exchange(core, "gx"))


def solution(mesh):
    in_specs = (P(None, "gx", "gy", "gz"), P(), P(), P(), P())
    out_specs = (P(), P("gx", "gy", "gz", None))
    return jax.shard_map(per_device, mesh=mesh, in_specs=in_specs, out_specs=out_specs, check_vma=False)
```

```python
import functools

import jax
import jax.numpy as jnp
from jax import lax
from jax.experimental import pallas as pl
from jax.experimental.pallas import tpu as pltpu
from jax.sharding import PartitionSpec as P

SUB = 3
R = 64
RV = 16
V = 32
CX = 24
CY = 48
CZ = 128
GX = 16
GZ = 8
HALF = CX // 2
EH = RV // 2
NX = 384
IPB = 3
EARLY = 9
STEP = 16
BLOCKS = ((0, 0), (0, 1), (0, 2), (1, 1), (1, 2), (2, 2))

f32 = jnp.float32
bf16 = jnp.bfloat16
highest = lax.Precision.HIGHEST


def iota(shape, dim):
    return lax.broadcasted_iota(jnp.int32, shape, dim)


def onehot(condition):
    return jnp.where(condition, 1.0, 0.0).astype(bf16)


def dot(a, b, contract=(1, 0), precision=None):
    return lax.dot_general(
        a, b, (((contract[0],), (contract[1],)), ((), ())), precision=precision, preferred_element_type=f32
    )


def depth_kernel(
    first, count, field_ref, third_ref, vars_ref, keep_ref, send_ref, cells_ref, third_here, vars_here, mix_ref, cols_ref, left_ref, sems
):
    gy = lax.axis_index("gy")
    gz = lax.axis_index("gz")

    def fetch(chunk):
        source = field_ref.at[:, :, pl.ds(first + chunk * IPB, IPB)]
        return pltpu.make_async_copy(source, cells_ref.at[:, :, pl.ds(chunk * IPB, IPB)], sems.at[chunk])

    third_part = third_ref.at[:, pl.ds(pl.multiple_of(gz * CZ, CZ), CZ)]
    third_copy = pltpu.make_async_copy(third_part, third_here, sems.at[count // IPB])
    vars_copy = pltpu.make_async_copy(vars_ref, vars_here, sems.at[count // IPB + 1])
    third_copy.start()
    vars_copy.start()
    for chunk in range(count // IPB):
        fetch(chunk).start()

    rows = iota((128, RV), 0)
    pick_e = onehot((((rows >> 3) + EH * gy) & (RV - 1)) == iota((128, RV), 1))
    vars_copy.wait()
    wide = dot(pick_e, vars_here[...]).astype(bf16)
    spread = onehot(iota((V, 256), 0) == iota((V, 256), 1) >> 3)
    same_j = (iota((128, 256), 0) & 7) == (iota((128, 256), 1) & 7)
    mix_ref[...] = jnp.where(same_j, dot(wide, spread), 0.0).astype(bf16)
    lane = iota((R, 256), 1)
    spread = onehot(iota((R, 256), 0) == (lane >> 5) * 8 + (lane & 7))
    third_copy.wait()
    full = dot(third_here[...], spread, (0, 0))
    which = (iota((CZ, 256), 1) >> 3) & 3
    for e in range(4):
        cols_ref[e * CZ : (e + 1) * CZ, :] = jnp.where(which == e, full, 0.0).astype(bf16)

    def step(chunk, carry):
        fetch(chunk).wait()
        mix = mix_ref[...]
        for ip in range(IPB):
            for jb in range(CY // 16):
                tiles = [cells_ref[:, s, chunk * IPB + ip, jb * 16 : jb * 16 + 16, :] for s in range(2)]
                halves = []
                for h in range(2):
                    pieces = [tile[:, h * 8 : h * 8 + 8, :].reshape(256, CZ) for tile in tiles]
                    halves.append(dot(mix, jnp.concatenate(pieces, axis=1)).reshape(RV, 8, 2 * CZ))
                reduced = jnp.concatenate(halves, axis=1).astype(bf16)
                for e in range(RV):
                    for s in range(2):
                        top = ((e // 4 * 2 + s) * IPB + ip) * CY + jb * 16
                        left_ref[chunk % 2, top : top + 16, e % 4 * CZ : (e % 4 + 1) * CZ] = reduced[
                            e, :, s * CZ : (s + 1) * CZ
                        ]
        depth = dot(left_ref[chunk % 2], cols_ref[...]).reshape(4, 2, IPB, CY, 256)
        for n in range(4):
            half = (keep_ref, send_ref)[n // 2]
            half[:, pl.ds(chunk * IPB, IPB), :, n % 2 * 256 : (n % 2 + 1) * 256] = depth[n]
        return carry

    lax.fori_loop(0, count // IPB, step, 0)


def local_depth(field, third, weights, first, count):
    half = jax.ShapeDtypeStruct((2, count, CY, 512), f32)
    far = pl.BlockSpec(memory_space=pltpu.HBM)
    near = pl.BlockSpec(memory_space=pltpu.VMEM)
    return pl.pallas_call(
        functools.partial(depth_kernel, first, count),
        in_specs=[far, far, far],
        out_specs=[near, near],
        out_shape=[half, half],
        scratch_shapes=[
            pltpu.VMEM((V, 2, count, CY, CZ), bf16),
            pltpu.VMEM((R, CZ), bf16),
            pltpu.VMEM((RV, V), bf16),
            pltpu.VMEM((128, 256), bf16),
            pltpu.VMEM((512, 256), bf16),
            pltpu.VMEM((2, 8 * IPB * CY, 512), bf16),
            pltpu.SemaphoreType.DMA((count // IPB + 2,)),
        ],
        compiler_params=pltpu.CompilerParams(vmem_limit_bytes=28 * 2**20),
        cost_estimate=pl.CostEstimate(flops=count * 6 * 10**8, bytes_accessed=count * 2**20, transcendentals=0),
        name="depth",
    )(*(pltpu.with_memory_space_constraint(x, pltpu.HBM) for x in (field, third, weights)))


def split(x):
    high = x.astype(bf16)
    return high, (x - high.astype(f32)).astype(bf16)


def turn_lanes(tiles, slot):
    skewed = []
    for k in range(4):
        mixed = tiles[-k % 4]
        for q in range(1, 4):
            mixed = jnp.where(slot == q, tiles[(q - k) % 4], mixed)
        skewed.append(mixed if k == 0 else pltpu.roll(mixed, 128 - 32 * k, 1))
    turned = []
    for d in range(4):
        whole = skewed[d]
        for n in range(1, 4):
            whole = jnp.where(slot == n, skewed[(d - n) % 4], whole)
        turned.append(whole)
    return turned


def project_kernel(keep_ref, recv_ref, keep_late_ref, recv_late_ref, second_ref, across_ref, keep_out_ref, send_out_ref, across_here, sems):
    gy = lax.axis_index("gy")
    x_half = lax.axis_index("gz") & 1
    rows = iota((R, R), 0)
    rank = ((rows >> 1) & 1) * 32 + (rows & 1) * 16 + (rows >> 2)
    picked = dot(onehot(rank == iota((R, R), 1)), second_ref[...])
    swapped = jnp.concatenate([picked[:, CY:], picked[:, :CY]], axis=1)
    own = jnp.where(gy == 0, picked, swapped)
    weights = jnp.concatenate([own, own], axis=1).astype(bf16)
    slot = iota((R, 128), 1) >> 5

    def project(ip, store, keep_ref=keep_ref, recv_ref=recv_ref):
        sides = []
        for s in range(2):
            keep_high, keep_low = split(keep_ref[s, ip])
            recv_high, recv_low = split(recv_ref[s, ip])
            sides.append(dot(weights, jnp.concatenate([keep_high, recv_high, keep_low, recv_low], axis=0)))
        for t in range(2):
            tiles = [sides[n // 2][:, n % 2 * 256 + t * 128 : n % 2 * 256 + (t + 1) * 128] for n in range(4)]
            turned = turn_lanes(tiles, slot)
            for d in range(0, 4, 2):
                own = jnp.where(x_half == 0, turned[d], turned[d + 1])
                other = jnp.where(x_half == 0, turned[d + 1], turned[d])
                store(2 * t + d // 2, own, other)

    def leave(ip):
        return pltpu.make_async_copy(across_here.at[:, :, ip], across_ref.at[:, :, ip], sems.at[ip])

    def first_half(ip, carry):
        def store(y, own, other):
            across_here[y, 0, ip] = own
            across_here[y, 1, ip] = other

        project(ip, store)
        leave(ip).start()
        return carry

    def second_half(ip, carry):
        def store(y, own, other):
            keep_out_ref[y, ip] = own
            send_out_ref[y, ip] = other

        project(ip + HALF // 2, store)
        return carry

    def last_cells(ip, carry):
        def store(y, own, other):
            keep_out_ref[y, ip] = own
            send_out_ref[y, ip] = other

        project(ip + HALF // 2 - EARLY, store, keep_late_ref, recv_late_ref)
        return carry

    lax.fori_loop(0, HALF // 2, first_half, 0, unroll=3)
    lax.fori_loop(0, EARLY - HALF // 2, second_half, 0, unroll=3)
    lax.fori_loop(EARLY - HALF // 2, HALF // 2, last_cells, 0, unroll=3)
    for ip in range(HALF // 2):
        leave(ip).wait()


def local_projected(keep, recv, keep_late, recv_late, second):
    part = (HALF // 2, R, 128)
    near = pl.BlockSpec(memory_space=pltpu.VMEM)
    return pl.pallas_call(
        project_kernel,
        out_shape=[
            jax.ShapeDtypeStruct((4, 2, *part), f32),
            jax.ShapeDtypeStruct((4, *part), f32),
            jax.ShapeDtypeStruct((4, *part), f32),
        ],
        out_specs=[pl.BlockSpec(memory_space=pl.ANY), near, near],
        scratch_shapes=[pltpu.VMEM((4, 2, *part), f32), pltpu.SemaphoreType.DMA((HALF // 2,))],
        compiler_params=pltpu.CompilerParams(vmem_limit_bytes=16 * 2**20),
        cost_estimate=pl.CostEstimate(flops=10**9, bytes_accessed=8 * 2**20, transcendentals=0),
        name="projected",
    )(keep, recv, keep_late, recv_late, second)


def gram_kernel(rows_ref, keep_ref, send_ref, columns_ref):
    gy = lax.axis_index("gy")
    low_lanes = iota((GX * HALF, 128), 1) < 64
    for t in range(2):
        first = rows_ref[pl.ds(2 * t, GX * HALF, stride=4), :]
        second = rows_ref[pl.ds(2 * t + 1, GX * HALF, stride=4), :]
        sides = (
            jnp.where(low_lanes, first, pltpu.roll(second, 64, 1)),
            jnp.where(low_lanes, pltpu.roll(first, 64, 1), second),
        )
        for s in range(2):
            for g in range(GX):
                top = g * CX + s * HALF
                columns_ref[top : top + HALF, t * 128 : (t + 1) * 128] = sides[s][g * HALF : (g + 1) * HALF, :]
    parts = split3(columns_ref[...])
    blocks = []
    for r, c in BLOCKS:
        left = [part[r * 128 : (r + 1) * 128, :] for part in parts]
        right = [part[c * 128 : (c + 1) * 128, :] for part in parts]
        blocks.append(dot3(left, right, (1, 1)))
    for n in range(3):
        keep_ref[0, n * 128 : (n + 1) * 128, :] = jnp.where(gy == 0, blocks[n], blocks[n + 3])
        send_ref[0, n * 128 : (n + 1) * 128, :] = jnp.where(gy == 0, blocks[n + 3], blocks[n])
    low, high = columns_ref[:, :128], columns_ref[:, 128:]
    keep_ref[1] = jnp.where(gy == 0, low, high)
    send_ref[1] = jnp.where(gy == 0, high, low)


def local_gram(rows):
    half = jax.ShapeDtypeStruct((2, NX, 128), f32)
    return pl.pallas_call(
        gram_kernel,
        out_shape=[half, half],
        scratch_shapes=[pltpu.VMEM((NX, 256), f32)],
        compiler_params=pltpu.CompilerParams(vmem_limit_bytes=8 * 2**20),
        name="gram",
    )(rows)


def split3(x):
    high = x.astype(bf16)
    rest = x - high.astype(f32)
    middle = rest.astype(bf16)
    return high, middle, (rest - middle.astype(f32)).astype(bf16)


def dot3(left, right, contract=(1, 0)):
    n = left[0].shape[0]
    all3 = dot(jnp.concatenate(left, axis=0), right[0], contract)
    two = dot(jnp.concatenate(left[:2], axis=0), right[1], contract)
    one = dot(left[0], right[2], contract)
    return all3[:n] + (all3[n : 2 * n] + two[:n]) + (all3[2 * n :] + two[n:] + one)


def invert_lower(matrix):
    row = iota((R, 128), 0)
    work = jnp.concatenate([matrix, jnp.where(iota((R, R), 0) == iota((R, R), 1), 1.0, 0.0)], axis=1)
    done = []
    for p in range(0, R, STEP):
        base = p // 8 * 8
        below = work[base:]
        columns = [jnp.broadcast_to(below[:, p + t : p + t + 1], below.shape) for t in range(STEP)]
        rows = [work[p + t : p + t + 1] for t in range(STEP)]
        for t in range(STEP):
            at = p + t - base
            pivot = columns[t][at : at + 1]
            inverse = 1.0 / pivot
            done.append(rows[t] * lax.rsqrt(pivot))
            scaled = rows[t] * inverse
            for s in range(t + 1, STEP):
                rows[s] = rows[s] - columns[t][p + s - base : p + s - base + 1] * scaled
                columns[s] = columns[s] - columns[t] * (columns[s][at : at + 1] * inverse)
            below = below - columns[t] * scaled
        work = below if base == 0 else jnp.concatenate([work[:base], below], axis=0)
    return jnp.concatenate(done, axis=0)[:, R:]


def factor_kernel(own_ref, other_ref, start_ref, keep_ref, recv_ref, factor_ref, core_ref, high_ref, middle_ref, low_ref):
    gy = lax.axis_index("gy")
    parts_refs = (high_ref, middle_ref, low_ref)
    for n, (r, c) in enumerate(BLOCKS):
        rows = slice(n % 3 * 128, (n % 3 + 1) * 128)
        own, other = own_ref[rows, :], other_ref[rows, :]
        block = jnp.where(gy == n // 3, own, other)
        for ref, part in zip(parts_refs, split3(block)):
            ref[r * 128 : (r + 1) * 128, c * 128 : (c + 1) * 128] = part
        if r != c:
            for ref, part in zip(parts_refs, split3(block.T)):
                ref[c * 128 : (c + 1) * 128, r * 128 : (r + 1) * 128] = part
    gram = tuple(ref[...] for ref in parts_refs)
    basis = start_ref[...]
    for _ in range(SUB):
        product = dot3(split3(basis), gram)
        parts = split3(product)
        inner = dot3(parts, parts, (1, 1))
        basis = dot3(split3(invert_lower(inner)), parts)
    factor_ref[...] = basis
    keep, recv = keep_ref[1], recv_ref[1]
    low, high = jnp.where(gy == 0, keep, recv), jnp.where(gy == 0, recv, keep)
    low_lanes = iota((NX, 128), 1) < 64
    columns = (
        jnp.where(low_lanes, low, pltpu.roll(high, 64, 1)),
        jnp.where(low_lanes, pltpu.roll(low, 64, 1), high),
    )
    left = split(basis)
    for b in range(2):
        right = split(columns[b])
        both = dot(jnp.concatenate(left, axis=0), right[0])
        core = both[:R] + both[R:] + dot(left[0], right[1])
        for g in range(GX):
            core_ref[g, 4 * b : 4 * b + 4, :] = core[4 * g : 4 * g + 4, :]


def factor_and_core(own, other, start, keep, recv):
    return pl.pallas_call(
        factor_kernel,
        out_shape=[jax.ShapeDtypeStruct((R, NX), f32), jax.ShapeDtypeStruct((GX, 8, 128), f32)],
        scratch_shapes=[pltpu.VMEM((NX, NX), bf16)] * 3,
        compiler_params=pltpu.CompilerParams(vmem_limit_bytes=8 * 2**20),
        name="factor",
    )(own, other, start, keep, recv)


def order_kernel(core_ref, out_ref, turned_ref):
    for a in range(4):
        pieces = [core_ref[pl.ds(4 * b + a, GX, stride=8), :] for b in range(2)]
        turned_ref[...] = jnp.concatenate(pieces, axis=0).T
        for c in range(8):
            out_ref[a, c] = turned_ref[pl.ds(c, RV, stride=8), :]


def ordered(core):
    out = pl.pallas_call(
        order_kernel,
        out_shape=jax.ShapeDtypeStruct((4, 8, RV, 32), f32),
        scratch_shapes=[pltpu.VMEM((128, 32), f32)],
        compiler_params=pltpu.CompilerParams(vmem_limit_bytes=8 * 2**20),
        name="order",
    )(core.reshape(GX * 8, 128))
    return out.transpose(0, 3, 1, 2)


def swap(x):
    return lax.ppermute(x, "gy", [(0, 1), (1, 0)])


def swap_x(x):
    return lax.ppermute(x, "gz", [(n, n ^ 1) for n in range(GZ)])


def exchange_y(x):
    groups = [[2 * y + x for y in range(4)] for x in range(2)]
    return lax.all_to_all(x, "gz", 0, 0, tiled=True, axis_index_groups=groups)


def exchange(x, axes):
    return lax.all_to_all(x, axes, 0, 0, tiled=True)


def per_device(field, start_first, factor_second, factor_third, factor_vars):
    field = field.reshape(V, 2, HALF, CY, CZ)
    third, weights = factor_third.T, factor_vars.T
    keep, send = local_depth(field, third, weights, 0, EARLY)
    keep_late, send_late = local_depth(field, third, weights, EARLY, HALF - EARLY)
    across, keep, send = local_projected(keep, swap(send), keep_late, swap(send_late), factor_second.T)
    recv = swap_x(send)
    across = jnp.sum(exchange_y(across), axis=0)
    second = keep + recv
    recv = swap_x(across[1])
    second = jnp.sum(exchange_y(second), axis=0)
    projected = jnp.concatenate([across[0] + recv, second], axis=0)
    projected = projected.reshape(HALF, GX, 4, 128).transpose(1, 0, 2, 3).reshape(GX, HALF * 4, 128)
    rows = exchange(projected, "gx").reshape(GX * HALF * 4, 128)
    keep, send = local_gram(rows)
    recv = swap(send)
    gram = (keep[0] + recv[0]).reshape(16, 24, 128)
    gram = jnp.sum(exchange(gram, "gx"), axis=0)
    gram = jnp.sum(exchange(jnp.broadcast_to(gram, (8, 24, 128)), "gz"), axis=0)
    own = exchange(jnp.broadcast_to(gram, (16, 24, 128)), "gx").reshape(NX, 128)
    first_factor, core = factor_and_core(own, swap(own), start_first.T, keep, recv)
    return first_factor.T, ordered(exchange(core, "gx"))


def solution(mesh):
    in_specs = (P(None, "gx", "gy", "gz"), P(), P(), P(), P())
    out_specs = (P(), P("gx", "gy", "gz", None))
    return jax.shard_map(per_device, mesh=mesh, in_specs=in_specs, out_specs=out_specs, check_vma=False)
```
